256 devices in a mesh: branch: 4 (over y), seq: 64 (over x, z, core).
Axes of the slice: x: 4, y: 4, z: 8, core: 2. Of those that a mesh axis runs over, the one named last changes fastest.
Arguments:
- queries: bfloat16 [4, 2048, 40, 256], P('branch', 'seq'), may hold values from -6 to 6
- keys_values: bfloat16 [4, 8192, 40, 256], P('branch', 'seq'), may hold values from -6 to 6
- prompt_bank: bfloat16 [8, 512, 4096], P('branch', 'seq'), may hold values from -6 to 6
- prompt_lengths: int32 [8], replicated, may hold values from 16 to 512
- requests: int32 [4], replicated, may hold values from 0 to 7
- w_text: bfloat16 [4096, 40, 256], P('seq'), may hold values from -0.09375 to 0.09375
- q_gain: float32 [40, 128], replicated, may hold values from 1.2 to 2
- k_gain: float32 [40, 128], replicated, may hold values from 1.2 to 2
- cq_gain: float32 [40, 128], replicated, may hold values from 1.2 to 2
- ck_gain: float32 [40, 128], replicated, may hold values from 1.2 to 2
Outputs:
- self_out: bfloat16 [4, 2048, 5120], P('branch', 'seq')
- cross_out: bfloat16 [4, 2048, 5120], P('branch', 'seq')
The draws below stay inside these ranges and needn't reach their ends.
All inputs are finite; a program needn't handle non-finite values.
Results may differ from the reference program's by a relative error of at most 0.011.
Values may be sent and summed in bfloat16 or wider, within the bound.
No kernel may reach another device: no remote copies, remote signals or barrier semaphores. Data moves between devices by JAX's collectives and lax.ppermute only.
A program may use at most 128 MiB of HBM per device.

```python
import math
import jax
import jax.numpy as jnp
from jax import lax

HEADS = 40
HD = 128
TW = 4096
TEXT = 512
Q = 2048
S = 8192
NP = 8
N_BRANCH = 4


def touch_ends(entries, key, low, top_value):
    longest = entries.shape.index(max(entries.shape))
    spots = []
    for shift in (0, 1):
        where = [jax.random.randint(jax.random.fold_in(key, axis), (), 0, length) for axis, length in enumerate(entries.shape)]
        where[longest] = (where[longest] + shift) % entries.shape[longest]
        spots.append(tuple(where))
    return entries.at[spots[0]].set(low).at[spots[1]].set(top_value)


def steps_of(stream_key, extent, shards, least, top_value):
    level, own = 1.0, jax.random.fold_in(stream_key, 6)
    for position, shards_of in shards:
        steps = jnp.exp(jax.random.uniform(jax.random.fold_in(own, position), (shards_of,), jnp.float32, least / len(shards), top_value / len(shards)))
        level = level * jnp.repeat(steps, extent[position] // shards_of).reshape([-1 if axis == position else 1 for axis in range(len(extent))])
    return level


def noise(own_key, extent, width, reach, pieces=(), kind=jnp.bfloat16):
    loudness = steps_of(own_key, extent, pieces, -0.22, 0.18) if pieces else 1.0
    array = jax.random.normal(own_key, extent, jnp.float32) * width * loudness
    return jnp.minimum(jnp.maximum(array, -reach), reach).astype(kind)


def setup_inputs(seed: int = 0) -> dict:
    key_list = jax.random.split(jax.random.key(seed), 11)
    return {
        "queries": noise(key_list[0], (N_BRANCH, Q, HEADS, 2 * HD), 1.0, 6.0, ((0, 4), (1, 64))),
        "keys_values": noise(key_list[1], (N_BRANCH, S, HEADS, 2 * HD), 1.0, 6.0, ((0, 4), (1, 64))),
        "prompt_bank": noise(key_list[2], (NP, TEXT, TW), 1.0, 6.0, ((0, 4), (1, 64))),
        "prompt_lengths": touch_ends(jax.random.randint(key_list[3], (NP,), 16, TEXT + 1), jax.random.fold_in(key_list[3], 1), 16, TEXT).astype(jnp.int32),
        "requests": touch_ends(jax.random.randint(key_list[4], (N_BRANCH,), 0, NP), jax.random.fold_in(key_list[4], 1), 0, NP - 1).astype(jnp.int32),
        "w_text": noise(key_list[5], (TW, HEADS, 2 * HD), TW ** -0.5, 0.09375, ((0, 64),)),
        "q_gain": jnp.clip(jax.random.uniform(key_list[6], (HEADS, HD), jnp.float32, 1.2, 2.0), 1.2, 2.0),
        "k_gain": jnp.clip(jax.random.uniform(key_list[7], (HEADS, HD), jnp.float32, 1.2, 2.0), 1.2, 2.0),
        "cq_gain": jnp.clip(jax.random.uniform(key_list[8], (HEADS, HD), jnp.float32, 1.2, 2.0), 1.2, 2.0),
        "ck_gain": jnp.clip(jax.random.uniform(key_list[9], (HEADS, HD), jnp.float32, 1.2, 2.0), 1.2, 2.0),
    }


EPSILON = 1e-06

def head_norm(values, gains):
    values = values.astype(jnp.float32)
    return values * lax.rsqrt(lax.optimization_barrier(jnp.mean(values * values, axis=-1, keepdims=True)) + EPSILON) * gains

def attend(query_rows, key_rows, value_rows, live, scale):
    scores = jnp.dot(query_rows, key_rows.T, preferred_element_type=jnp.float32) * scale
    powers = jnp.exp(scores)
    if live is not None:
        powers = jnp.where(live[None, :], powers, jnp.float32(0.0))
    weights = (powers / lax.optimization_barrier(jnp.sum(powers, axis=-1, keepdims=True))).astype(jnp.bfloat16)
    return jnp.dot(weights, value_rows, preferred_element_type=jnp.float32).astype(jnp.bfloat16)

def reference(queries, keys_values, prompt_bank, prompt_lengths, requests, w_text, q_gain, k_gain, cq_gain, ck_gain):
    scale = 1.0 / math.sqrt(HD)
    self_groups = []
    cross_groups = []
    for group in range(N_BRANCH):
        self_queries = head_norm(queries[group, :, :, :HD], q_gain).astype(jnp.bfloat16)
        cross_queries = head_norm(queries[group, :, :, HD:], cq_gain).astype(jnp.bfloat16)
        self_keys = head_norm(keys_values[group, :, :, :HD], k_gain).astype(jnp.bfloat16)
        self_values = keys_values[group, :, :, HD:]
        prompt_id = requests[group].astype(jnp.int32)
        context = lax.dynamic_index_in_dim(prompt_bank, prompt_id, 0, keepdims=False)
        length = lax.dynamic_index_in_dim(prompt_lengths, prompt_id, 0, keepdims=False)
        live = jnp.arange(TEXT, dtype=jnp.int32) < length

        def per_head(head):
            weights = lax.dynamic_index_in_dim(w_text, head, 1, keepdims=False)
            projected = jnp.dot(context, weights, preferred_element_type=jnp.float32)
            key_gain = lax.dynamic_index_in_dim(ck_gain, head, 0, keepdims=False)
            text_keys = head_norm(projected[:, :HD], key_gain).astype(jnp.bfloat16)
            text_values = projected[:, HD:].astype(jnp.bfloat16)
            own_self = lax.dynamic_index_in_dim(self_queries, head, 1, keepdims=False)
            own_cross = lax.dynamic_index_in_dim(cross_queries, head, 1, keepdims=False)
            own_keys = lax.dynamic_index_in_dim(self_keys, head, 1, keepdims=False)
            own_values = lax.dynamic_index_in_dim(self_values, head, 1, keepdims=False)
            self_part = attend(own_self, own_keys, own_values, None, scale)
            cross_part = attend(own_cross, text_keys, text_values, live, scale)
            return (self_part, cross_part)
        self_heads, cross_heads = lax.map(per_head, jnp.arange(HEADS, dtype=jnp.int32))
        self_groups.append(jnp.transpose(self_heads, (1, 0, 2)).reshape(Q, HEADS * HD))
        cross_groups.append(jnp.transpose(cross_heads, (1, 0, 2)).reshape(Q, HEADS * HD))
    return (jnp.stack(self_groups), jnp.stack(cross_groups))
```

```python
import functools
import math

import jax
import jax.numpy as jnp
from jax import lax
from jax.experimental import pallas as pl
from jax.experimental.pallas import tpu as pltpu
from jax.sharding import Mesh
from jax.sharding import PartitionSpec as P

EPSILON = 1e-06
BF16 = jnp.bfloat16
F32 = jnp.float32
NX, NZ, NC = 4, 8, 2
GROUP = ("x", "c")


def head_norm(values, gains):
    values = values.astype(F32)
    return values * lax.rsqrt(jnp.mean(values * values, axis=-1, keepdims=True) + EPSILON) * gains


def ring(size, step):
    return [(i, (i + step) % size) for i in range(size)]


def columns_to_rows(sums):
    eye = lax.broadcasted_iota(jnp.int32, (128, 128), 0) == lax.broadcasted_iota(
        jnp.int32, (128, 128), 1
    )
    return [
        jnp.sum(jnp.where(eye, sums[a * 128 : (a + 1) * 128], 0.0), axis=0, keepdims=True)
        for a in range(sums.shape[0] // 128)
    ]


def self_kernel(order, q_ref, k_ref, v_ref, *refs, chunks, rows, keys, scale):
    q_refs = (q_ref,) + refs[: chunks - 1]
    o_ref, l_ref = refs[chunks - 1 :]
    values = v_ref[...].reshape(1024, 256)[:, 128:]
    values = jnp.concatenate([values, jnp.ones((1024, 128), BF16)], axis=1)
    queries = jnp.concatenate([ref[...].reshape(256, 128) for ref in q_refs], axis=0)
    for i in range(chunks * 256 // rows):
        part = queries[i * rows : (i + 1) * rows]
        total = None
        for j in range(1024 // keys):
            scores = lax.dot_general(
                part,
                k_ref[0, j * keys : (j + 1) * keys],
                (((1,), (1,)), ((), ())),
                preferred_element_type=F32,
            )
            powers = jnp.exp2(scores * scale).astype(BF16)
            term = jnp.dot(
                powers, values[j * keys : (j + 1) * keys], preferred_element_type=F32
            )
            total = term if total is None else total + term
        for a in range(rows // 256):
            chunk = i * rows // 256 + a
            piece = total[a * 256 : (a + 1) * 256]
            o_ref[chunk] = piece[:, :128].reshape(8, 1, 32, 128).astype(o_ref.dtype)
            l_ref[chunk, 0] = jnp.concatenate(
                columns_to_rows(piece[:, 128:]) + [jnp.zeros((6, 128), F32)], axis=0
            )


def self_part(order, gathered, keys, pairs, scale, out_type):
    chunks = order.shape[0]
    slots = keys.shape[0]

    def q_spec(n):
        return pl.BlockSpec((1, 8, 1, 32, 128), lambda h, order: (order[n], 0, h, 0, 0))

    grid_spec = pltpu.PrefetchScalarGridSpec(
        num_scalar_prefetch=1,
        grid=(slots,),
        in_specs=[
            q_spec(0),
            pl.BlockSpec((1, 1024, 128), lambda h, order: (h, 0, 0)),
            pl.BlockSpec((8, 1, 128, 256), lambda h, order: (0, h, 0, 0)),
        ]
        + [q_spec(n) for n in range(1, chunks)],
        out_specs=[
            pl.BlockSpec((chunks, 8, 1, 32, 128), lambda h, order: (0, 0, h, 0, 0)),
            pl.BlockSpec((chunks, 1, 8, 128), lambda h, order: (0, h, 0, 0)),
        ],
    )
    pairs_count = slots * chunks * 256 * 1024
    return pl.pallas_call(
        functools.partial(
            self_kernel, chunks=chunks, rows=256 * chunks, keys=512, scale=scale
        ),
        grid_spec=grid_spec,
        out_shape=[
            jax.ShapeDtypeStruct((chunks, 8, slots, 32, 128), out_type),
            jax.ShapeDtypeStruct((chunks, slots, 8, 128), F32),
        ],
        compiler_params=pltpu.CompilerParams(vmem_limit_bytes=48 << 20),
        cost_estimate=pl.CostEstimate(
            flops=pairs_count * 128 * 6, bytes_accessed=6 << 20, transcendentals=pairs_count
        ),
        name="self_part",
    )(order, gathered, keys, pairs, *([gathered] * (chunks - 1)))


def norm_kernel(kv_ref, gain_ref, out_ref):
    keys = kv_ref[...].reshape(1024, 256)[:, :128]
    out_ref[0] = head_norm(keys, gain_ref[0]).astype(BF16)


def norm_keys(pairs, gains):
    slots = pairs.shape[1]
    return pl.pallas_call(
        norm_kernel,
        grid=(slots,),
        in_specs=[
            pl.BlockSpec((8, 1, 128, 256), lambda h: (0, h, 0, 0)),
            pl.BlockSpec((1, 1, 128), lambda h: (h, 0, 0)),
        ],
        out_specs=pl.BlockSpec((1, 1024, 128), lambda h: (h, 0, 0)),
        out_shape=jax.ShapeDtypeStruct((slots, 1024, 128), BF16),
        compiler_params=pltpu.CompilerParams(vmem_limit_bytes=48 << 20),
        name="norm_keys",
    )(pairs, gains[:, None, :])


def cross_kernel(q_ref, text_ref, live_ref, o_ref, *, scale):
    text = text_ref[...].reshape(512, 256)
    queries = q_ref[...].reshape(256, 128)
    scores = lax.dot_general(
        queries, text[:, :128], (((1,), (1,)), ((), ())), preferred_element_type=F32
    )
    powers = jnp.where(live_ref[...] > 0.0, jnp.exp2(scores * scale), 0.0)
    weights = powers / jnp.sum(powers, axis=1, keepdims=True)
    result = jnp.dot(weights.astype(BF16), text[:, 128:], preferred_element_type=F32)
    o_ref[...] = result.astype(BF16).reshape(8, 1, 32, 128)


def cross_part(queries, text, live, scale):
    slots = queries.shape[1]
    return pl.pallas_call(
        functools.partial(cross_kernel, scale=scale),
        grid=(slots,),
        in_specs=[
            pl.BlockSpec((8, 1, 32, 128), lambda h: (0, h, 0, 0)),
            pl.BlockSpec((8, 1, 64, 256), lambda h: (0, h, 0, 0)),
            pl.BlockSpec((1, 512), lambda h: (0, 0)),
        ],
        out_specs=pl.BlockSpec((8, 1, 32, 128), lambda h: (0, h, 0, 0)),
        out_shape=jax.ShapeDtypeStruct(queries.shape, BF16),
        compiler_params=pltpu.CompilerParams(vmem_limit_bytes=48 << 20),
        name="cross_part",
    )(queries, text, live)


def local(
    queries,
    keys_values,
    prompt_bank,
    prompt_lengths,
    requests,
    w_text,
    q_gain,
    k_gain,
    cq_gain,
    ck_gain,
):
    branch = lax.axis_index("branch")
    x = lax.axis_index("x")
    z = lax.axis_index("z")
    c = lax.axis_index("c")
    heads, head_dim = q_gain.shape
    slots = heads // (NX * NC)
    scale = math.log2(math.e) / math.sqrt(head_dim)
    tokens = queries.shape[1]

    def head_major(values):
        return jnp.transpose(values, (1, 0, 2)).reshape(
            8, slots, values.shape[0], values.shape[2]
        )

    local_queries = queries[0]
    self_queries = head_major(head_norm(local_queries[..., :head_dim], q_gain).astype(BF16))
    self_queries = lax.all_to_all(self_queries, GROUP, 0, 0, tiled=True)
    gathered = lax.all_gather(self_queries, "z", axis=0)

    pairs = lax.all_to_all(head_major(keys_values[0]), GROUP, 0, 0, tiled=True)
    group = x * NC + c
    my_gains = lax.dynamic_slice_in_dim(k_gain, group * slots, slots, 0)
    keys = norm_keys(pairs, my_gains)

    per_branch = prompt_bank.shape[0]
    held = requests // per_branch == branch
    picked = jnp.take(prompt_bank, jnp.remainder(requests, per_branch), axis=0)
    outgoing = jnp.where(held[:, None, None], picked, jnp.zeros_like(picked))
    incoming = lax.all_to_all(outgoing, "branch", split_axis=0, concat_axis=0, tiled=True)
    source = jnp.take(requests, branch) // per_branch
    rows = lax.dynamic_index_in_dim(incoming, source, 0, keepdims=False)
    count = rows.shape[0]
    rows = rows.reshape(count, NX, NZ, NC, 4, 16)
    rows = jnp.transpose(rows, (1, 3, 0, 4, 2, 5)).reshape(8, count, 512)
    rows = lax.all_to_all(rows, GROUP, 0, 0, tiled=True).reshape(8 * count, 512)
    context = lax.all_gather(rows, "z", axis=0)

    part = lax.dynamic_slice_in_dim(w_text, branch * 16, 16, 0)
    part = lax.all_to_all(head_major(part), "z", 0, 0, tiled=True)
    planes = [part] + [lax.ppermute(part, "branch", ring(4, k)) for k in (1, 2, 3)]
    planes = jnp.stack(planes + planes)
    planes = jnp.flip(planes, 0)
    weights = lax.dynamic_slice_in_dim(planes, 3 - branch, 4, 0)

    partial = jnp.einsum(
        "btk,hkc->bhtc",
        context,
        jnp.transpose(weights, (2, 0, 1, 3, 4)).reshape(slots, 512, 2 * head_dim),
        preferred_element_type=F32,
    ).astype(BF16)
    projected = lax.psum_scatter(partial, GROUP, scatter_dimension=0, tiled=True)[0]
    text_gains = lax.dynamic_slice_in_dim(ck_gain, z * slots, slots, 0)
    text_keys = head_norm(projected[..., :head_dim], text_gains[:, None, :]).astype(BF16)
    text = jnp.concatenate([text_keys, projected[..., head_dim:]], axis=-1)
    text = lax.all_gather(text, GROUP, axis=0)

    entry = jnp.arange(512, dtype=jnp.int32)
    of_z, of_x, of_c, of_row = entry // 64, entry // 16 % 4, entry // 8 % 2, entry % 8
    text_row = ((of_x * NZ + of_z) * NC + of_c) * 8 + of_row
    prompt_length = jnp.take(prompt_lengths, jnp.take(requests, branch))
    live = (text_row < prompt_length).astype(F32)[None, :]

    cross_queries = head_major(head_norm(local_queries[..., head_dim:], cq_gain).astype(BF16))
    cross_queries = lax.all_to_all(cross_queries, "z", 0, 0, tiled=True)
    cross = cross_part(cross_queries, text, live, scale)
    cross = lax.all_to_all(cross, "z", 0, 0, tiled=True)

    def chunk_order(*steps):
        return jnp.stack([(z + step) % NZ for step in steps]).astype(jnp.int32)

    far, far_sums = self_part(chunk_order(4), gathered, keys, pairs, scale, BF16)
    right = lax.ppermute(far[0, :4], "z", ring(NZ, 1))
    left = lax.ppermute(far[0, 4:], "z", ring(NZ, -1))
    sums = {4: far_sums[0]}
    for step in (3, 2, 1):
        own, own_sums = self_part(chunk_order(step, -step), gathered, keys, pairs, scale, F32)
        sums[step], sums[8 - step] = own_sums[0], own_sums[1]
        if step == 3:
            to_right = jnp.concatenate([own[0, :4] + right.astype(F32), own[0, 4:]], axis=0)
            to_left = jnp.concatenate([own[1, :4], own[1, 4:] + left.astype(F32)], axis=0)
        else:
            to_right = own[0] + right.astype(F32)
            to_left = own[1] + left.astype(F32)
        right = lax.ppermute(to_right.astype(BF16), "z", ring(NZ, 1))
        left = lax.ppermute(to_left.astype(BF16), "z", ring(NZ, -1))
    own, own_sums = self_part(chunk_order(0), gathered, keys, pairs, scale, F32)
    sums[0] = own_sums[0]
    by_step = jnp.stack([sums[k] for k in range(8)])[:, :, :2]
    by_step = jnp.concatenate([by_step, by_step], axis=0)
    by_chunk = lax.dynamic_slice_in_dim(by_step, NZ - z, NZ, 0)
    total = jnp.sum(lax.all_to_all(by_chunk, "z", 0, 0, tiled=True), axis=0)
    total = jnp.transpose(total.reshape(slots, 8, 32), (1, 0, 2))[..., None]
    mine = (own[0] + right.astype(F32) + left.astype(F32)) / total
    mine = lax.all_to_all(mine.astype(BF16), GROUP, 0, 0, tiled=True)

    def token_major(values):
        values = values.reshape(heads, tokens, head_dim)
        return jnp.transpose(values, (1, 0, 2)).reshape(1, tokens, heads * head_dim)

    return token_major(mine), token_major(cross)


def solution(mesh):
    fine = Mesh(mesh.devices.reshape(4, NX, NZ, NC), ("branch", "x", "z", "c"))
    seq = ("x", "z", "c")
    in_specs = (
        P("branch", seq, None, None),
        P("branch", seq, None, None),
        P("branch", seq, None),
        P(),
        P(),
        P(seq, None, None),
        P(),
        P(),
        P(),
        P(),
    )
    out_specs = (P("branch", seq, None), P("branch", seq, None))
    return jax.shard_map(local, mesh=fine, in_specs=in_specs, out_specs=out_specs, check_vma=False)
```

```python
import functools
import math

import jax
import jax.numpy as jnp
from jax import lax
from jax.experimental import pallas as pl
from jax.experimental.pallas import tpu as pltpu
from jax.sharding import Mesh
from jax.sharding import PartitionSpec as P

EPSILON = 1e-06
BF16 = jnp.bfloat16
F32 = jnp.float32
NX, NZ, NC = 4, 8, 2
GROUP = ("x", "c")
SUMS = 16
ROWS = 256
VMEM = 24 << 20
ALL_VMEM = 60 << 20


def head_norm(values, gains):
    values = values.astype(F32)
    return values * lax.rsqrt(jnp.mean(values * values, axis=-1, keepdims=True) + EPSILON) * gains


def ring(size, step):
    return [(i, (i + step) % size) for i in range(size)]


def eye_mask():
    first = lax.broadcasted_iota(jnp.int32, (128, 128), 0)
    return first == lax.broadcasted_iota(jnp.int32, (128, 128), 1)


def self_kernel(q_ref, kv_ref, o_ref, *, rows, keys, scale):
    pairs = kv_ref[...].reshape(1024, 256)
    values = jnp.concatenate([pairs[:, 128:], jnp.ones((1024, 128), BF16)], axis=1)
    queries = q_ref[...].reshape(NZ * ROWS, 128)
    eye = eye_mask()
    for i in range(NZ * ROWS // rows):
        total = None
        for j in range(1024 // keys):
            scores = lax.dot_general(
                queries[i * rows : (i + 1) * rows],
                pairs[j * keys : (j + 1) * keys, :128],
                (((1,), (1,)), ((), ())),
                preferred_element_type=F32,
            )
            powers = jnp.exp2(scores * scale).astype(BF16)
            term = jnp.dot(powers, values[j * keys : (j + 1) * keys], preferred_element_type=F32)
            total = term if total is None else total + term
        for a in range(rows // ROWS):
            piece = total[a * ROWS : (a + 1) * ROWS]
            sums = [
                jnp.sum(jnp.where(eye, piece[b * 128 : (b + 1) * 128, 128:], 0.0), axis=0, keepdims=True)
                for b in range(2)
            ]
            sums = jnp.concatenate(sums + [jnp.zeros((6, 128), F32)], axis=0)
            high = sums.astype(BF16).astype(F32)
            result = jnp.concatenate([high, sums - high, piece[:, :128]], axis=0)
            o_ref[i * rows // ROWS + a, 0] = result.astype(BF16)


def self_part(gathered, pairs, scale):
    slots = pairs.shape[1]
    pairs_count = slots * NZ * ROWS * 1024
    return pl.pallas_call(
        functools.partial(self_kernel, rows=512, keys=512, scale=scale),
        grid=(slots,),
        in_specs=[
            pl.BlockSpec((NZ, 8, 32, 128), lambda h: (0, 0, h, 0)),
            pl.BlockSpec((8, 1, 128, 256), lambda h: (0, h, 0, 0)),
        ],
        out_specs=pl.BlockSpec((NZ, 1, SUMS + ROWS, 128), lambda h: (0, h, 0, 0)),
        out_shape=jax.ShapeDtypeStruct((NZ, slots, SUMS + ROWS, 128), BF16),
        compiler_params=pltpu.CompilerParams(vmem_limit_bytes=ALL_VMEM),
        cost_estimate=pl.CostEstimate(
            flops=pairs_count * 128 * 6, bytes_accessed=6 << 20, transcendentals=pairs_count
        ),
        name="self_part",
    )(gathered, pairs)


def last_kernel(total_ref, out_ref):
    eye = eye_mask()
    for h in range(out_ref.shape[1]):
        sums = total_ref[h, :SUMS].astype(F32)
        sums = sums[:8] + sums[8:]
        for b in range(2):
            rows = slice(SUMS + b * 128, SUMS + (b + 1) * 128)
            line = jnp.broadcast_to(sums[b : b + 1], (128, 128))
            column = jnp.sum(jnp.where(eye, line, 0.0), axis=1, keepdims=True)
            value = total_ref[h, rows].astype(F32)
            out_ref[b * 4 : (b + 1) * 4, h] = (value / column).astype(BF16).reshape(4, 32, 128)


def last_part(total):
    slots = total.shape[0]
    return pl.pallas_call(
        last_kernel,
        out_shape=jax.ShapeDtypeStruct((8, slots, 32, 128), BF16),
        compiler_params=pltpu.CompilerParams(vmem_limit_bytes=VMEM),
        name="last_part",
    )(total)


def norm_kernel(kv_ref, gain_ref, out_ref):
    out_ref[..., :128] = head_norm(kv_ref[..., :128], gain_ref[...]).astype(BF16)
    out_ref[..., 128:] = kv_ref[..., 128:]


def norm_keys(pairs, gains):
    heads, rows, width = pairs.shape
    block = heads // 8
    return pl.pallas_call(
        norm_kernel,
        grid=(8,),
        in_specs=[
            pl.BlockSpec((block, rows, width), lambda g: (g, 0, 0)),
            pl.BlockSpec((block, 1, 128), lambda g: (g, 0, 0)),
        ],
        out_specs=pl.BlockSpec((block, rows, width), lambda g: (g, 0, 0)),
        out_shape=jax.ShapeDtypeStruct(pairs.shape, BF16),
        compiler_params=pltpu.CompilerParams(vmem_limit_bytes=VMEM),
        name="norm_keys",
    )(pairs, gains[:, None, :])


def nothing(*refs):
    del refs


def after(value, *others):
    anywhere = pl.BlockSpec(memory_space=pl.ANY)
    return pl.pallas_call(
        nothing,
        in_specs=[anywhere] * (1 + len(others)),
        out_specs=anywhere,
        out_shape=jax.ShapeDtypeStruct(value.shape, value.dtype),
        input_output_aliases={0: 0},
        name="after",
    )(value, *others)


def pick_kernel(which_ref, b0, b1, b2, b3, out_ref):
    plane, prompt = which_ref[0], which_ref[1]
    rows = None
    for k, ref in enumerate((b0, b1, b2, b3)):
        for p in range(ref.shape[0]):
            value = ref[p].astype(F32)
            here = jnp.logical_and(plane == k, prompt == p)
            rows = value if rows is None else jnp.where(here, value, rows)
    count = rows.shape[0]
    rows = rows.astype(BF16)
    for x in range(NX):
        for block in range(8):
            first = (x * 8 + block) * 128
            for c in range(NC):
                at = slice(block * count, (block + 1) * count)
                out_ref[x * NC + c, at] = rows[:, first : first + 128]


def pick_part(which, banks):
    per_branch, count, width = banks[0].shape
    return pl.pallas_call(
        pick_kernel,
        grid_spec=pltpu.PrefetchScalarGridSpec(
            num_scalar_prefetch=1,
            grid=(1,),
            in_specs=[pl.BlockSpec(banks[0].shape, lambda i, w: (0, 0, 0))] * 4,
            out_specs=pl.BlockSpec((8, 8 * count, 128), lambda i, w: (0, 0, 0)),
        ),
        out_shape=jax.ShapeDtypeStruct((8, 8 * count, 128), BF16),
        compiler_params=pltpu.CompilerParams(vmem_limit_bytes=VMEM),
        name="pick_part",
    )(which, *banks)


def text_sum_kernel(where_ref, p0, p1, p2, p3, gain_ref, out_ref):
    total = p0[...].astype(F32)
    for ref in (p1, p2, p3):
        total = total + ref[...].astype(F32)
    keys = head_norm(total, gain_ref[0])
    out_ref[...] = jnp.where(where_ref[3] == 0, keys, total).astype(BF16)


def text_sum(where, parts, gains):
    slots, rows, width = parts[0].shape
    return pl.pallas_call(
        text_sum_kernel,
        grid_spec=pltpu.PrefetchScalarGridSpec(
            num_scalar_prefetch=1,
            grid=(1,),
            in_specs=[pl.BlockSpec((slots, rows, width), lambda i, w: (0, 0, 0))] * 4
            + [pl.BlockSpec((1, slots, 1, width), lambda i, w: (w[1], 0, 0, 0))],
            out_specs=pl.BlockSpec((slots, rows, width), lambda i, w: (0, 0, 0)),
        ),
        out_shape=jax.ShapeDtypeStruct((slots, rows, width), BF16),
        compiler_params=pltpu.CompilerParams(vmem_limit_bytes=VMEM),
        name="text_sum",
    )(where, *parts, gains.reshape(NZ, slots, 1, width))


def text_kernel(where_ref, low_ref, high_ref, w0, w1, w2, w3, o0, o1, o2, o3, held, context):
    branch, z, x, c = where_ref[0], where_ref[1], where_ref[2], where_ref[3]
    for k, ref in enumerate((w0, w1, w2, w3)):
        held[lax.rem(branch - k + 4, 4)] = ref[:, :, 0]
    weights = jnp.concatenate(
        [
            held[plane, lax.rem(of_c + c, NC), lax.rem(z - of_z + NZ, NZ)]
            for of_z in range(NZ)
            for of_c in range(NC)
            for plane in range(4)
        ],
        axis=0,
    )

    @pl.when(pl.program_id(0) == 0)
    def _():
        for i, ref in enumerate((low_ref, high_ref)):
            rows = ref[...].astype(F32)
            for j in range(4):
                part = rows[:, :, j * 8 : (j + 1) * 8].reshape(512, 128)
                first = (i * 4 + j) * 128
                context[:, first : first + 128] = part.astype(BF16)

    for k, ref in enumerate((o0, o1, o2, o3)):
        first = pl.multiple_of(lax.rem(x + k, NX) * 128, 128)
        result = jnp.dot(context[pl.ds(first, 128)], weights, preferred_element_type=F32)
        ref[0] = result.astype(BF16)


def text_part(where, gathered, weights):
    slots = weights[0].shape[2]
    first = slots
    grid_spec = pltpu.PrefetchScalarGridSpec(
        num_scalar_prefetch=1,
        grid=(slots,),
        in_specs=[
            pl.BlockSpec((NZ, 8, 32, 128), lambda h, w: (0, 0, first, 0)),
            pl.BlockSpec((NZ, 8, 32, 128), lambda h, w: (0, 0, first + 1, 0)),
        ]
        + [pl.BlockSpec((NC, NZ, 1, 16, 128), lambda h, w: (0, 0, h, 0, 0))] * 4,
        out_specs=[pl.BlockSpec((1, 128, 128), lambda h, w: (h, 0, 0))] * NX,
        scratch_shapes=[pltpu.VMEM((4, NC, NZ, 16, 128), BF16), pltpu.VMEM((512, 1024), BF16)],
    )
    return pl.pallas_call(
        text_kernel,
        grid_spec=grid_spec,
        out_shape=[jax.ShapeDtypeStruct((slots, 128, 128), BF16)] * NX,
        compiler_params=pltpu.CompilerParams(vmem_limit_bytes=ALL_VMEM),
        name="text_part",
    )(where, gathered, gathered, *weights)


def cross_kernel(where_ref, q_ref, mine_ref, other_ref, live_ref, o_ref, *, scale):
    mine, other = mine_ref[...].reshape(512, 128), other_ref[...].reshape(512, 128)
    first = where_ref[3] == 0
    keys, values = jnp.where(first, mine, other), jnp.where(first, other, mine)
    queries = q_ref[...].reshape(ROWS, 128)
    scores = lax.dot_general(
        queries, keys, (((1,), (1,)), ((), ())), preferred_element_type=F32
    )
    powers = jnp.where(live_ref[...] > 0.0, jnp.exp2(scores * scale), 0.0)
    weights = powers / jnp.sum(powers, axis=1, keepdims=True)
    result = jnp.dot(weights.astype(BF16), values, preferred_element_type=F32)
    o_ref[...] = result.astype(BF16).reshape(8, 1, 32, 128)


def cross_part(where, queries, mine, other, live, scale):
    slots = queries.shape[1]
    half = pl.BlockSpec((NX, 1, 128, 128), lambda h, w: (0, h, 0, 0))
    grid_spec = pltpu.PrefetchScalarGridSpec(
        num_scalar_prefetch=1,
        grid=(slots,),
        in_specs=[
            pl.BlockSpec((8, 1, 32, 128), lambda h, w: (0, h, 0, 0)),
            half,
            half,
            pl.BlockSpec((1, 512), lambda h, w: (0, 0)),
        ],
        out_specs=pl.BlockSpec((8, 1, 32, 128), lambda h, w: (0, h, 0, 0)),
    )
    return pl.pallas_call(
        functools.partial(cross_kernel, scale=scale),
        grid_spec=grid_spec,
        out_shape=jax.ShapeDtypeStruct(queries.shape, BF16),
        compiler_params=pltpu.CompilerParams(vmem_limit_bytes=VMEM),
        name="cross_part",
    )(where, queries, mine, other, live)


def local(
    queries,
    keys_values,
    prompt_bank,
    prompt_lengths,
    requests,
    w_text,
    q_gain,
    k_gain,
    cq_gain,
    ck_gain,
):
    branch = lax.axis_index("branch")
    z = lax.axis_index("z")
    x = lax.axis_index("x")
    c = lax.axis_index("c")
    where = jnp.stack([branch, z, x, c]).astype(jnp.int32)
    heads, head_dim = q_gain.shape
    slots = heads // (NX * NC)
    scale = math.log2(math.e) / math.sqrt(head_dim)
    tokens = queries.shape[1]
    per_branch, count, width = prompt_bank.shape

    def head_major(values):
        return jnp.transpose(values, (1, 0, 2)).reshape(
            8, slots, values.shape[0], values.shape[2]
        )

    wanted = jnp.take(requests, branch)
    which = jnp.stack([(branch - wanted // per_branch) % 4, wanted % per_branch])
    banks = [prompt_bank] + [lax.ppermute(prompt_bank, "branch", ring(4, k)) for k in (1, 2, 3)]
    columns = pick_part(which.astype(jnp.int32), banks)

    local_queries = queries[0]
    self_queries = head_major(head_norm(local_queries[..., :head_dim], q_gain).astype(BF16))
    self_queries = self_queries.reshape(8, slots * tokens, 128)
    got = lax.all_to_all(
        jnp.concatenate([self_queries, columns], axis=1), GROUP, 0, 0, tiled=True
    )

    pairs = norm_keys(jnp.transpose(keys_values[0], (1, 0, 2)), k_gain)
    got = after(got, pairs)
    pairs = pairs.reshape(8, slots, keys_values.shape[1], 2 * head_dim)
    pairs = lax.all_to_all(pairs, GROUP, 0, 0, tiled=True)
    gathered = lax.all_gather(got, "z", axis=0)

    part = after(head_major(lax.dynamic_slice_in_dim(w_text, branch * 16, 16, 0)), got)
    moved = [lax.dynamic_index_in_dim(part, z, 0, keepdims=False)]
    for k in range(1, NZ):
        piece = lax.dynamic_index_in_dim(part, (z + k) % NZ, 0, keepdims=False)
        moved.append(lax.ppermute(piece, "z", ring(NZ, k)))
    moved = jnp.stack(moved)
    halves = moved[..., :head_dim], moved[..., head_dim:]
    mine = jnp.where(c == 0, halves[0], halves[1])
    other = lax.ppermute(jnp.where(c == 0, halves[1], halves[0]), "c", ring(NC, 1))
    moved = jnp.stack([mine, other])
    weights = [moved] + [lax.ppermute(moved, "branch", ring(4, k)) for k in (1, 2, 3)]

    cross_queries = head_major(head_norm(local_queries[..., head_dim:], cq_gain).astype(BF16))
    cross_queries = lax.all_to_all(after(cross_queries, pairs), "z", 0, 0, tiled=True)

    entry = jnp.arange(512, dtype=jnp.int32)
    of_z = 2 * ((x - entry // 128 + NX) % NX) + entry % 128 // 64
    of_x, of_c, of_row = entry // 16 % 4, entry // 8 % 2, entry % 8
    text_row = ((of_x * NZ + of_z) * NC + of_c) * 8 + of_row
    live = (text_row < jnp.take(prompt_lengths, wanted)).astype(F32)[None, :]

    def to_others(pieces):
        return [pieces[0]] + [lax.ppermute(pieces[k], "x", ring(NX, k)) for k in (1, 2, 3)]

    gathered = after(gathered, cross_queries, *weights)
    own = self_part(gathered, pairs, scale)
    total = lax.psum_scatter(own, "z", scatter_dimension=0)

    parts = to_others(text_part(where, after(gathered, own), weights))
    text = jnp.stack(to_others([text_sum(where, parts, ck_gain)] * NX))
    other = lax.ppermute(text, "c", ring(NC, 1))
    cross = cross_part(where, cross_queries, text, other, live, scale)
    cross = lax.all_to_all(cross, "z", 0, 0, tiled=True)
    mine = last_part(total)
    mine = lax.all_to_all(mine, GROUP, 0, 0, tiled=True)

    def token_major(values):
        values = values.reshape(heads, tokens, head_dim)
        return jnp.transpose(values, (1, 0, 2)).reshape(1, tokens, heads * head_dim)

    return token_major(mine), token_major(cross)


def solution(mesh):
    fine = Mesh(mesh.devices.reshape(4, NX, NZ, NC), ("branch", "x", "z", "c"))
    seq = ("x", "z", "c")
    in_specs = (
        P("branch", seq, None, None),
        P("branch", seq, None, None),
        P("branch", seq, None),
        P(),
        P(),
        P(seq, None, None),
        P(),
        P(),
        P(),
        P(),
    )
    out_specs = (P("branch", seq, None), P("branch", seq, None))
    return jax.shard_map(local, mesh=fine, in_specs=in_specs, out_specs=out_specs, check_vma=False)
```

```python
import functools
import math

import jax
import jax.numpy as jnp
from jax import lax
from jax.experimental import pallas as pl
from jax.experimental.pallas import tpu as pltpu
from jax.sharding import Mesh
from jax.sharding import PartitionSpec as P

EPSILON = 1e-06
BF16 = jnp.bfloat16
F32 = jnp.float32
NX, NZ, NC = 4, 8, 2
GROUP = ("x", "c")
SUMS = 16
ROWS = 256
VMEM = 24 << 20
ALL_VMEM = 60 << 20


def head_norm(values, gains):
    values = values.astype(F32)
    return values * lax.rsqrt(jnp.mean(values * values, axis=-1, keepdims=True) + EPSILON) * gains


def ring(size, step):
    return [(i, (i + step) % size) for i in range(size)]


def eye_mask():
    first = lax.broadcasted_iota(jnp.int32, (128, 128), 0)
    return first == lax.broadcasted_iota(jnp.int32, (128, 128), 1)


def self_kernel(q_ref, kv_ref, o_ref, *, rows, keys, scale):
    pairs = kv_ref[...].reshape(1024, 256)
    values = jnp.concatenate([pairs[:, 128:], jnp.ones((1024, 128), BF16)], axis=1)
    queries = q_ref[...].reshape(NZ * ROWS, 128)
    eye = eye_mask()
    for i in range(NZ * ROWS // rows):
        total = None
        for j in range(1024 // keys):
            scores = lax.dot_general(
                queries[i * rows : (i + 1) * rows],
                pairs[j * keys : (j + 1) * keys, :128],
                (((1,), (1,)), ((), ())),
                preferred_element_type=F32,
            )
            powers = jnp.exp2(scores * scale).astype(BF16)
            term = jnp.dot(powers, values[j * keys : (j + 1) * keys], preferred_element_type=F32)
            total = term if total is None else total + term
        for a in range(rows // ROWS):
            piece = total[a * ROWS : (a + 1) * ROWS]
            sums = [
                jnp.sum(jnp.where(eye, piece[b * 128 : (b + 1) * 128, 128:], 0.0), axis=0, keepdims=True)
                for b in range(2)
            ]
            sums = jnp.concatenate(sums + [jnp.zeros((6, 128), F32)], axis=0)
            high = sums.astype(BF16).astype(F32)
            result = jnp.concatenate([high, sums - high, piece[:, :128]], axis=0)
            o_ref[i * rows // ROWS + a, 0] = result.astype(BF16)


def self_part(gathered, pairs, scale):
    slots = pairs.shape[1]
    pairs_count = slots * NZ * ROWS * 1024
    return pl.pallas_call(
        functools.partial(self_kernel, rows=512, keys=512, scale=scale),
        grid=(slots,),
        in_specs=[
            pl.BlockSpec((NZ, 8, 32, 128), lambda h: (0, 0, h, 0)),
            pl.BlockSpec((8, 1, 128, 256), lambda h: (0, h, 0, 0)),
        ],
        out_specs=pl.BlockSpec((NZ, 1, SUMS + ROWS, 128), lambda h: (0, h, 0, 0)),
        out_shape=jax.ShapeDtypeStruct((NZ, slots, SUMS + ROWS, 128), BF16),
        compiler_params=pltpu.CompilerParams(vmem_limit_bytes=ALL_VMEM),
        cost_estimate=pl.CostEstimate(
            flops=pairs_count * 128 * 6, bytes_accessed=6 << 20, transcendentals=pairs_count
        ),
        name="self_part",
    )(gathered, pairs)


def last_kernel(total_ref, out_ref):
    eye = eye_mask()
    for h in range(out_ref.shape[1]):
        sums = total_ref[h, :SUMS].astype(F32)
        sums = sums[:8] + sums[8:]
        for b in range(2):
            rows = slice(SUMS + b * 128, SUMS + (b + 1) * 128)
            line = jnp.broadcast_to(sums[b : b + 1], (128, 128))
            column = jnp.sum(jnp.where(eye, line, 0.0), axis=1, keepdims=True)
            value = total_ref[h, rows].astype(F32)
            out_ref[b * 4 : (b + 1) * 4, h] = (value / column).astype(BF16).reshape(4, 32, 128)


def last_part(total):
    slots = total.shape[0]
    return pl.pallas_call(
        last_kernel,
        out_shape=jax.ShapeDtypeStruct((8, slots, 32, 128), BF16),
        compiler_params=pltpu.CompilerParams(vmem_limit_bytes=VMEM),
        name="last_part",
    )(total)


def norm_kernel(kv_ref, gain_ref, out_ref):
    out_ref[..., :128] = head_norm(kv_ref[..., :128], gain_ref[...]).astype(BF16)
    out_ref[..., 128:] = kv_ref[..., 128:]


def norm_keys(pairs, gains):
    heads, rows, width = pairs.shape
    block = heads // 8
    return pl.pallas_call(
        norm_kernel,
        grid=(8,),
        in_specs=[
            pl.BlockSpec((block, rows, width), lambda g: (g, 0, 0)),
            pl.BlockSpec((block, 1, 128), lambda g: (g, 0, 0)),
        ],
        out_specs=pl.BlockSpec((block, rows, width), lambda g: (g, 0, 0)),
        out_shape=jax.ShapeDtypeStruct(pairs.shape, BF16),
        compiler_params=pltpu.CompilerParams(vmem_limit_bytes=VMEM),
        name="norm_keys",
    )(pairs, gains[:, None, :])


def nothing(*refs):
    del refs


def after(value, *others):
    anywhere = pl.BlockSpec(memory_space=pl.ANY)
    return pl.pallas_call(
        nothing,
        in_specs=[anywhere] * (1 + len(others)),
        out_specs=anywhere,
        out_shape=jax.ShapeDtypeStruct(value.shape, value.dtype),
        input_output_aliases={0: 0},
        name="after",
    )(value, *others)


def pick_kernel(where_ref, requests_ref, b0, b1, b2, b3, out_ref):
    wanted = requests_ref[where_ref[0]]
    per_branch = b0.shape[0]
    plane = lax.rem(where_ref[0] - wanted // per_branch + 4, 4)
    prompt = lax.rem(wanted, per_branch)
    rows = None
    for k, ref in enumerate((b0, b1, b2, b3)):
        for p in range(ref.shape[0]):
            value = ref[p].astype(F32)
            here = jnp.logical_and(plane == k, prompt == p)
            rows = value if rows is None else jnp.where(here, value, rows)
    count = rows.shape[0]
    rows = rows.astype(BF16)
    for x in range(NX):
        for block in range(8):
            first = (x * 8 + block) * 128
            for c in range(NC):
                at = slice(block * count, (block + 1) * count)
                out_ref[x * NC + c, at] = rows[:, first : first + 128]


def pick_part(where, requests, banks):
    per_branch, count, width = banks[0].shape
    return pl.pallas_call(
        pick_kernel,
        grid_spec=pltpu.PrefetchScalarGridSpec(
            num_scalar_prefetch=2,
            grid=(1,),
            in_specs=[pl.BlockSpec(banks[0].shape, lambda i, w, r: (0, 0, 0))] * 4,
            out_specs=pl.BlockSpec((8, 8 * count, 128), lambda i, w, r: (0, 0, 0)),
        ),
        out_shape=jax.ShapeDtypeStruct((8, 8 * count, 128), BF16),
        compiler_params=pltpu.CompilerParams(vmem_limit_bytes=VMEM),
        name="pick_part",
    )(where, requests, *banks)


def text_sum_kernel(where_ref, p0, p1, p2, p3, gain_ref, out_ref):
    total = p0[...].astype(F32)
    for ref in (p1, p2, p3):
        total = total + ref[...].astype(F32)
    keys = head_norm(total, gain_ref[0])
    out_ref[...] = jnp.where(where_ref[3] == 0, keys, total).astype(BF16)


def text_sum(where, parts, gains):
    slots, rows, width = parts[0].shape
    return pl.pallas_call(
        text_sum_kernel,
        grid_spec=pltpu.PrefetchScalarGridSpec(
            num_scalar_prefetch=1,
            grid=(1,),
            in_specs=[pl.BlockSpec((slots, rows, width), lambda i, w: (0, 0, 0))] * 4
            + [pl.BlockSpec((1, slots, 1, width), lambda i, w: (w[1], 0, 0, 0))],
            out_specs=pl.BlockSpec((slots, rows, width), lambda i, w: (0, 0, 0)),
        ),
        out_shape=jax.ShapeDtypeStruct((slots, rows, width), BF16),
        compiler_params=pltpu.CompilerParams(vmem_limit_bytes=VMEM),
        name="text_sum",
    )(where, *parts, gains.reshape(NZ, slots, 1, width))


def text_kernel(where_ref, low_ref, high_ref, w0, w1, w2, w3, o0, o1, o2, o3, held, context, product):
    branch, z, x, c = where_ref[0], where_ref[1], where_ref[2], where_ref[3]
    for k, ref in enumerate((w0, w1, w2, w3)):
        held[lax.rem(branch - k + 4, 4)] = ref[...]
    for i, ref in enumerate((low_ref, high_ref)):
        rows = ref[...].astype(F32)
        for j in range(4):
            part = rows[:, :, j * 8 : (j + 1) * 8].reshape(512, 128)
            first = (i * 4 + j) * 128
            context[:, first : first + 128] = part.astype(BF16)
    for h in range(held.shape[3]):
        weights = jnp.concatenate(
            [
                held[plane, lax.rem(of_c + c, NC), lax.rem(z - of_z + NZ, NZ), h]
                for of_z in range(NZ)
                for of_c in range(NC)
                for plane in range(4)
            ],
            axis=0,
        )
        result = jnp.dot(context[...], weights, preferred_element_type=F32)
        product[:, h] = result.astype(BF16).reshape(NX, 128, 128)
    for k, ref in enumerate((o0, o1, o2, o3)):
        ref[...] = product[lax.rem(x + k, NX)]


def text_part(where, gathered, weights):
    slots = weights[0].shape[2]
    first = slots
    grid_spec = pltpu.PrefetchScalarGridSpec(
        num_scalar_prefetch=1,
        grid=(1,),
        in_specs=[
            pl.BlockSpec((NZ, 8, 32, 128), lambda i, w: (0, 0, first, 0)),
            pl.BlockSpec((NZ, 8, 32, 128), lambda i, w: (0, 0, first + 1, 0)),
        ]
        + [pl.BlockSpec(weights[0].shape, lambda i, w: (0, 0, 0, 0, 0))] * 4,
        out_specs=[pl.BlockSpec((slots, 128, 128), lambda i, w: (0, 0, 0))] * NX,
        scratch_shapes=[
            pltpu.VMEM((4,) + weights[0].shape, BF16),
            pltpu.VMEM((512, 1024), BF16),
            pltpu.VMEM((NX, slots, 128, 128), BF16),
        ],
    )
    return pl.pallas_call(
        text_kernel,
        grid_spec=grid_spec,
        out_shape=[jax.ShapeDtypeStruct((slots, 128, 128), BF16)] * NX,
        compiler_params=pltpu.CompilerParams(vmem_limit_bytes=ALL_VMEM),
        name="text_part",
    )(where, gathered, gathered, *weights)


def cross_kernel(where_ref, requests_ref, lengths_ref, q_ref, mine_ref, other_ref, o_ref, *, scale):
    entry = lax.broadcasted_iota(jnp.int32, (1, 512), 1)
    of_z = 2 * jnp.bitwise_and(where_ref[2] - (entry >> 7) + NX, NX - 1) + ((entry >> 6) & 1)
    of_x, of_c, of_row = (entry >> 4) & 3, (entry >> 3) & 1, entry & 7
    text_row = ((of_x * NZ + of_z) * NC + of_c) * 8 + of_row
    live = text_row < lengths_ref[requests_ref[where_ref[0]]]
    mine, other = mine_ref[...].reshape(512, 128), other_ref[...].reshape(512, 128)
    first = where_ref[3] == 0
    keys, values = jnp.where(first, mine, other), jnp.where(first, other, mine)
    queries = q_ref[...].reshape(ROWS, 128)
    scores = lax.dot_general(
        queries, keys, (((1,), (1,)), ((), ())), preferred_element_type=F32
    )
    powers = jnp.where(live, jnp.exp2(scores * scale), 0.0)
    weights = powers / jnp.sum(powers, axis=1, keepdims=True)
    result = jnp.dot(weights.astype(BF16), values, preferred_element_type=F32)
    result = result.astype(BF16).reshape(8, 32, 128)
    for of_z in range(NZ):
        o_ref[lax.rem(where_ref[1] - of_z + NZ, NZ), 0] = result[of_z]


def cross_part(where, requests, lengths, queries, mine, other, scale):
    slots = queries.shape[1]
    half = pl.BlockSpec((NX, 1, 128, 128), lambda h, *refs: (0, h, 0, 0))
    grid_spec = pltpu.PrefetchScalarGridSpec(
        num_scalar_prefetch=3,
        grid=(slots,),
        in_specs=[pl.BlockSpec((8, 1, 32, 128), lambda h, *refs: (0, h, 0, 0)), half, half],
        out_specs=pl.BlockSpec((8, 1, 32, 128), lambda h, *refs: (0, h, 0, 0)),
    )
    return pl.pallas_call(
        functools.partial(cross_kernel, scale=scale),
        grid_spec=grid_spec,
        out_shape=jax.ShapeDtypeStruct(queries.shape, BF16),
        compiler_params=pltpu.CompilerParams(vmem_limit_bytes=VMEM),
        name="cross_part",
    )(where, requests, lengths, queries, mine, other)


def place_kernel(where_ref, *refs):
    out_ref = refs[-1]
    slots, _, width = refs[0].shape
    for k, ref in enumerate(refs[:-1]):
        first = lax.rem(where_ref[1] + k, NZ) * (slots * width)
        for h in range(slots):
            at = pl.multiple_of(first + h * width, 128)
            out_ref[:, pl.ds(at, width)] = ref[h]


def place_part(where, pieces):
    slots, rows, width = pieces[0].shape
    return pl.pallas_call(
        place_kernel,
        grid_spec=pltpu.PrefetchScalarGridSpec(
            num_scalar_prefetch=1,
            grid=(1,),
            in_specs=[pl.BlockSpec((slots, rows, width), lambda i, w: (0, 0, 0))] * NZ,
            out_specs=pl.BlockSpec((rows, NZ * slots * width), lambda i, w: (0, 0)),
        ),
        out_shape=jax.ShapeDtypeStruct((rows, NZ * slots * width), BF16),
        compiler_params=pltpu.CompilerParams(vmem_limit_bytes=VMEM),
        name="place_part",
    )(where, *pieces)


def local(
    queries,
    keys_values,
    prompt_bank,
    prompt_lengths,
    requests,
    w_text,
    q_gain,
    k_gain,
    cq_gain,
    ck_gain,
):
    branch = lax.axis_index("branch")
    z = lax.axis_index("z")
    x = lax.axis_index("x")
    c = lax.axis_index("c")
    where = jnp.stack([branch, z, x, c]).astype(jnp.int32)
    heads, head_dim = q_gain.shape
    slots = heads // (NX * NC)
    scale = math.log2(math.e) / math.sqrt(head_dim)
    tokens = queries.shape[1]
    per_branch, count, width = prompt_bank.shape

    def head_major(values):
        return jnp.transpose(values, (1, 0, 2)).reshape(
            8, slots, values.shape[0], values.shape[2]
        )

    banks = [prompt_bank] + [lax.ppermute(prompt_bank, "branch", ring(4, k)) for k in (1, 2, 3)]
    columns = pick_part(where, requests, banks)

    local_queries = queries[0]
    self_queries = head_major(head_norm(local_queries[..., :head_dim], q_gain).astype(BF16))
    self_queries = self_queries.reshape(8, slots * tokens, 128)
    got = lax.all_to_all(
        jnp.concatenate([self_queries, columns], axis=1), GROUP, 0, 0, tiled=True
    )

    pairs = norm_keys(jnp.transpose(keys_values[0], (1, 0, 2)), k_gain)
    got = after(got, pairs)
    pairs = pairs.reshape(8, slots, keys_values.shape[1], 2 * head_dim)
    pairs = lax.all_to_all(pairs, GROUP, 0, 0, tiled=True)
    gathered = lax.all_gather(got, "z", axis=0)

    part = after(head_major(lax.dynamic_slice_in_dim(w_text, branch * 16, 16, 0)), got)
    moved = [lax.dynamic_index_in_dim(part, z, 0, keepdims=False)]
    for k in range(1, NZ):
        piece = lax.dynamic_index_in_dim(part, (z + k) % NZ, 0, keepdims=False)
        moved.append(lax.ppermute(piece, "z", ring(NZ, k)))
    moved = jnp.stack(moved)
    halves = moved[..., :head_dim], moved[..., head_dim:]
    mine = jnp.where(c == 0, halves[0], halves[1])
    other = lax.ppermute(jnp.where(c == 0, halves[1], halves[0]), "c", ring(NC, 1))
    moved = jnp.stack([mine, other])
    weights = [moved] + [lax.ppermute(moved, "branch", ring(4, k)) for k in (1, 2, 3)]

    def to_others(pieces):
        return [pieces[0]] + [lax.ppermute(pieces[k], "x", ring(NX, k)) for k in (1, 2, 3)]

    gathered = after(gathered, *weights)
    own = self_part(gathered, pairs, scale)
    total = lax.psum_scatter(own, "z", scatter_dimension=0)

    cross_queries = head_major(head_norm(local_queries[..., head_dim:], cq_gain).astype(BF16))
    cross_queries = lax.all_to_all(after(cross_queries, own), "z", 0, 0, tiled=True)

    parts = to_others(text_part(where, after(gathered, own), weights))
    parts[0] = after(parts[0], cross_queries)
    text = jnp.stack(to_others([text_sum(where, parts, ck_gain)] * NX))
    other = lax.ppermute(text, "c", ring(NC, 1))
    cross = cross_part(where, requests, prompt_lengths, cross_queries, text, other, scale)
    cross = [cross[0]] + [lax.ppermute(cross[k], "z", ring(NZ, -k)) for k in range(1, NZ)]
    cross = place_part(where, cross)
    mine = last_part(total)
    mine = lax.all_to_all(mine, GROUP, 0, 0, tiled=True)

    def token_major(values):
        values = values.reshape(heads, tokens, head_dim)
        return jnp.transpose(values, (1, 0, 2)).reshape(1, tokens, heads * head_dim)

    return token_major(mine), cross[None]


def solution(mesh):
    fine = Mesh(mesh.devices.reshape(4, NX, NZ, NC), ("branch", "x", "z", "c"))
    seq = ("x", "z", "c")
    in_specs = (
        P("branch", seq, None, None),
        P("branch", seq, None, None),
        P("branch", seq, None),
        P(),
        P(),
        P(seq, None, None),
        P(),
        P(),
        P(),
        P(),
    )
    out_specs = (P("branch", seq, None), P("branch", seq, None))
    return jax.shard_map(local, mesh=fine, in_specs=in_specs, out_specs=out_specs, check_vma=False)
```

```python
import functools
import math

import jax
import jax.numpy as jnp
from jax import lax
from jax.experimental import pallas as pl
from jax.experimental.pallas import tpu as pltpu
from jax.sharding import Mesh
from jax.sharding import PartitionSpec as P

EPSILON = 1e-06
BF16 = jnp.bfloat16
F32 = jnp.float32
NX, NZ, NC = 4, 8, 2
GROUP = ("x", "c")
SUMS = 16
ROWS = 256
VMEM = 24 << 20
ALL_VMEM = 60 << 20


def head_norm(values, gains):
    values = values.astype(F32)
    return values * lax.rsqrt(jnp.mean(values * values, axis=-1, keepdims=True) + EPSILON) * gains


def ring(size, step):
    return [(i, (i + step) % size) for i in range(size)]


def eye_mask():
    first = lax.broadcasted_iota(jnp.int32, (128, 128), 0)
    return first == lax.broadcasted_iota(jnp.int32, (128, 128), 1)


def self_kernel(q_ref, kv_ref, o_ref, *, rows, keys, scale):
    pairs = kv_ref[...].reshape(1024, 256)
    values = jnp.concatenate([pairs[:, 128:], jnp.ones((1024, 128), BF16)], axis=1)
    queries = q_ref[...].reshape(NZ * ROWS, 128)
    eye = eye_mask()
    for i in range(NZ * ROWS // rows):
        total = None
        for j in range(1024 // keys):
            scores = lax.dot_general(
                queries[i * rows : (i + 1) * rows],
                pairs[j * keys : (j + 1) * keys, :128],
                (((1,), (1,)), ((), ())),
                preferred_element_type=F32,
            )
            powers = jnp.exp2(scores * scale).astype(BF16)
            term = jnp.dot(powers, values[j * keys : (j + 1) * keys], preferred_element_type=F32)
            total = term if total is None else total + term
        for a in range(rows // ROWS):
            piece = total[a * ROWS : (a + 1) * ROWS]
            sums = [
                jnp.sum(jnp.where(eye, piece[b * 128 : (b + 1) * 128, 128:], 0.0), axis=0, keepdims=True)
                for b in range(2)
            ]
            sums = jnp.concatenate(sums + [jnp.zeros((6, 128), F32)], axis=0)
            high = sums.astype(BF16).astype(F32)
            result = jnp.concatenate([high, sums - high, piece[:, :128]], axis=0)
            o_ref[i * rows // ROWS + a, 0] = result.astype(BF16)


def self_part(gathered, pairs, scale):
    slots = pairs.shape[1]
    pairs_count = slots * NZ * ROWS * 1024
    return pl.pallas_call(
        functools.partial(self_kernel, rows=1024, keys=1024, scale=scale),
        grid=(slots,),
        in_specs=[
            pl.BlockSpec((NZ, 8, 32, 128), lambda h: (0, 0, h, 0)),
            pl.BlockSpec((8, 1, 128, 256), lambda h: (0, h, 0, 0)),
        ],
        out_specs=pl.BlockSpec((NZ, 1, SUMS + ROWS, 128), lambda h: (0, h, 0, 0)),
        out_shape=jax.ShapeDtypeStruct((NZ, slots, SUMS + ROWS, 128), BF16),
        compiler_params=pltpu.CompilerParams(vmem_limit_bytes=ALL_VMEM),
        cost_estimate=pl.CostEstimate(
            flops=pairs_count * 128 * 6, bytes_accessed=6 << 20, transcendentals=pairs_count
        ),
        name="self_part",
    )(gathered, pairs)


def last_kernel(total_ref, out_ref):
    eye = eye_mask()
    for h in range(out_ref.shape[1]):
        sums = total_ref[h, :SUMS].astype(F32)
        sums = sums[:8] + sums[8:]
        for b in range(2):
            rows = slice(SUMS + b * 128, SUMS + (b + 1) * 128)
            line = jnp.broadcast_to(sums[b : b + 1], (128, 128))
            column = jnp.sum(jnp.where(eye, line, 0.0), axis=1, keepdims=True)
            value = total_ref[h, rows].astype(F32)
            out_ref[b * 4 : (b + 1) * 4, h] = (value / column).astype(BF16).reshape(4, 32, 128)


def last_part(total):
    slots = total.shape[0]
    return pl.pallas_call(
        last_kernel,
        out_shape=jax.ShapeDtypeStruct((8, slots, 32, 128), BF16),
        compiler_params=pltpu.CompilerParams(vmem_limit_bytes=ALL_VMEM),
        name="last_part",
    )(total)


def norm_kernel(kv_ref, gain_ref, out_ref):
    out_ref[..., :128] = head_norm(kv_ref[..., :128], gain_ref[...]).astype(BF16)
    out_ref[..., 128:] = kv_ref[..., 128:]


def norm_keys(pairs, gains):
    heads, rows, width = pairs.shape
    block = heads // 8
    return pl.pallas_call(
        norm_kernel,
        grid=(8,),
        in_specs=[
            pl.BlockSpec((block, rows, width), lambda g: (g, 0, 0)),
            pl.BlockSpec((block, 1, 128), lambda g: (g, 0, 0)),
        ],
        out_specs=pl.BlockSpec((block, rows, width), lambda g: (g, 0, 0)),
        out_shape=jax.ShapeDtypeStruct(pairs.shape, BF16),
        compiler_params=pltpu.CompilerParams(vmem_limit_bytes=VMEM),
        name="norm_keys",
    )(pairs, gains[:, None, :])


def nothing(*refs):
    del refs


def after(value, *others):
    anywhere = pl.BlockSpec(memory_space=pl.ANY)
    return pl.pallas_call(
        nothing,
        in_specs=[anywhere] * (1 + len(others)),
        out_specs=anywhere,
        out_shape=jax.ShapeDtypeStruct(value.shape, value.dtype),
        input_output_aliases={0: 0},
        name="after",
    )(value, *others)


def pick_kernel(where_ref, requests_ref, b0, b1, b2, b3, out_ref):
    wanted = requests_ref[where_ref[0]]
    per_branch = b0.shape[0]
    plane = lax.rem(where_ref[0] - wanted // per_branch + 4, 4)
    prompt = lax.rem(wanted, per_branch)
    rows = None
    for k, ref in enumerate((b0, b1, b2, b3)):
        for p in range(ref.shape[0]):
            value = ref[p].astype(F32)
            here = jnp.logical_and(plane == k, prompt == p)
            rows = value if rows is None else jnp.where(here, value, rows)
    count = rows.shape[0]
    rows = rows.astype(BF16)
    for x in range(NX):
        for block in range(8):
            first = (x * 8 + block) * 128
            for c in range(NC):
                at = slice(block * count, (block + 1) * count)
                out_ref[x * NC + c, at] = rows[:, first : first + 128]


def pick_part(where, requests, banks):
    per_branch, count, width = banks[0].shape
    return pl.pallas_call(
        pick_kernel,
        grid_spec=pltpu.PrefetchScalarGridSpec(
            num_scalar_prefetch=2,
            grid=(1,),
            in_specs=[pl.BlockSpec(banks[0].shape, lambda i, w, r: (0, 0, 0))] * 4,
            out_specs=pl.BlockSpec((8, 8 * count, 128), lambda i, w, r: (0, 0, 0)),
        ),
        out_shape=jax.ShapeDtypeStruct((8, 8 * count, 128), BF16),
        compiler_params=pltpu.CompilerParams(vmem_limit_bytes=VMEM),
        name="pick_part",
    )(where, requests, *banks)


def text_sum_kernel(where_ref, p0, p1, p2, p3, gain_ref, out_ref):
    total = p0[...].astype(F32)
    for ref in (p1, p2, p3):
        total = total + ref[...].astype(F32)
    keys = head_norm(total, gain_ref[0])
    out_ref[...] = jnp.where(where_ref[3] == 0, keys, total).astype(BF16)


def text_sum(where, parts, gains):
    slots, rows, width = parts[0].shape
    return pl.pallas_call(
        text_sum_kernel,
        grid_spec=pltpu.PrefetchScalarGridSpec(
            num_scalar_prefetch=1,
            grid=(1,),
            in_specs=[pl.BlockSpec((slots, rows, width), lambda i, w: (0, 0, 0))] * 4
            + [pl.BlockSpec((1, slots, 1, width), lambda i, w: (w[1], 0, 0, 0))],
            out_specs=pl.BlockSpec((slots, rows, width), lambda i, w: (0, 0, 0)),
        ),
        out_shape=jax.ShapeDtypeStruct((slots, rows, width), BF16),
        compiler_params=pltpu.CompilerParams(vmem_limit_bytes=VMEM),
        name="text_sum",
    )(where, *parts, gains.reshape(NZ, slots, 1, width))


def text_kernel(where_ref, low_ref, high_ref, w0, w1, w2, w4, w3, o0, o1, o2, o3, held, context, product):
    branch, z, x, c = where_ref[0], where_ref[1], where_ref[2], where_ref[3]
    for k, ref in ((0, w0), (1, w1), (3, w3)):
        held[lax.rem(branch - k + 4, 4)] = ref[...]
    for i, ref in enumerate((w2, w4)):
        held[lax.rem(branch + 2, 4), i] = ref[...]
    for i, ref in enumerate((low_ref, high_ref)):
        rows = ref[...].astype(F32)
        for j in range(4):
            part = rows[:, :, j * 8 : (j + 1) * 8].reshape(512, 128)
            first = (i * 4 + j) * 128
            context[:, first : first + 128] = part.astype(BF16)
    for h in range(held.shape[3]):
        weights = jnp.concatenate(
            [
                held[plane, lax.rem(of_c + c, NC), lax.rem(z - of_z + NZ, NZ), h]
                for of_z in range(NZ)
                for of_c in range(NC)
                for plane in range(4)
            ],
            axis=0,
        )
        result = jnp.dot(context[...], weights, preferred_element_type=F32)
        product[:, h] = result.astype(BF16).reshape(NX, 128, 128)
    for k, ref in enumerate((o0, o1, o2, o3)):
        ref[...] = product[lax.rem(x + k, NX)]


def text_part(where, gathered, weights):
    slots = weights[0].shape[2]
    first = slots
    grid_spec = pltpu.PrefetchScalarGridSpec(
        num_scalar_prefetch=1,
        grid=(1,),
        in_specs=[
            pl.BlockSpec((NZ, 8, 32, 128), lambda i, w: (0, 0, first, 0)),
            pl.BlockSpec((NZ, 8, 32, 128), lambda i, w: (0, 0, first + 1, 0)),
        ]
        + [
            pl.BlockSpec(value.shape, lambda i, w, n=value.ndim: (0,) * n) for value in weights
        ],
        out_specs=[pl.BlockSpec((slots, 128, 128), lambda i, w: (0, 0, 0))] * NX,
        scratch_shapes=[
            pltpu.VMEM((4,) + weights[0].shape, BF16),
            pltpu.VMEM((512, 1024), BF16),
            pltpu.VMEM((NX, slots, 128, 128), BF16),
        ],
    )
    return pl.pallas_call(
        text_kernel,
        grid_spec=grid_spec,
        out_shape=[jax.ShapeDtypeStruct((slots, 128, 128), BF16)] * NX,
        compiler_params=pltpu.CompilerParams(vmem_limit_bytes=ALL_VMEM),
        name="text_part",
    )(where, gathered, gathered, *weights)


def cross_kernel(where_ref, requests_ref, lengths_ref, q_ref, mine_ref, other_ref, o_ref, *, scale):
    entry = lax.broadcasted_iota(jnp.int32, (1, 512), 1)
    of_z = 2 * jnp.bitwise_and(where_ref[2] - (entry >> 7) + NX, NX - 1) + ((entry >> 6) & 1)
    of_x, of_c, of_row = (entry >> 4) & 3, (entry >> 3) & 1, entry & 7
    text_row = ((of_x * NZ + of_z) * NC + of_c) * 8 + of_row
    live = text_row < lengths_ref[requests_ref[where_ref[0]]]
    mine, other = mine_ref[...].reshape(512, 128), other_ref[...].reshape(512, 128)
    first = where_ref[3] == 0
    keys, values = jnp.where(first, mine, other), jnp.where(first, other, mine)
    queries = q_ref[...].reshape(ROWS, 128)
    scores = lax.dot_general(
        queries, keys, (((1,), (1,)), ((), ())), preferred_element_type=F32
    )
    powers = jnp.where(live, jnp.exp2(scores * scale), 0.0)
    weights = powers / jnp.sum(powers, axis=1, keepdims=True)
    result = jnp.dot(weights.astype(BF16), values, preferred_element_type=F32)
    result = result.astype(BF16).reshape(8, 32, 128)
    for of_z in range(NZ):
        o_ref[lax.rem(where_ref[1] - of_z + NZ, NZ), 0] = result[of_z]


def cross_part(where, requests, lengths, queries, mine, other, scale):
    slots = queries.shape[1]
    half = pl.BlockSpec((NX, 1, 128, 128), lambda h, *refs: (0, h, 0, 0))
    grid_spec = pltpu.PrefetchScalarGridSpec(
        num_scalar_prefetch=3,
        grid=(slots,),
        in_specs=[pl.BlockSpec((8, 1, 32, 128), lambda h, *refs: (0, h, 0, 0)), half, half],
        out_specs=pl.BlockSpec((8, 1, 32, 128), lambda h, *refs: (0, h, 0, 0)),
    )
    return pl.pallas_call(
        functools.partial(cross_kernel, scale=scale),
        grid_spec=grid_spec,
        out_shape=jax.ShapeDtypeStruct(queries.shape, BF16),
        compiler_params=pltpu.CompilerParams(vmem_limit_bytes=VMEM),
        name="cross_part",
    )(where, requests, lengths, queries, mine, other)


def place_kernel(where_ref, *refs):
    out_ref = refs[-1]
    slots, _, width = refs[0].shape
    for k, ref in enumerate(refs[:-1]):
        first = lax.rem(where_ref[1] + k, NZ) * (slots * width)
        for h in range(slots):
            at = pl.multiple_of(first + h * width, 128)
            out_ref[:, pl.ds(at, width)] = ref[h]


def place_part(where, pieces):
    slots, rows, width = pieces[0].shape
    return pl.pallas_call(
        place_kernel,
        grid_spec=pltpu.PrefetchScalarGridSpec(
            num_scalar_prefetch=1,
            grid=(1,),
            in_specs=[pl.BlockSpec((slots, rows, width), lambda i, w: (0, 0, 0))] * NZ,
            out_specs=pl.BlockSpec((rows, NZ * slots * width), lambda i, w: (0, 0)),
        ),
        out_shape=jax.ShapeDtypeStruct((rows, NZ * slots * width), BF16),
        compiler_params=pltpu.CompilerParams(vmem_limit_bytes=VMEM),
        name="place_part",
    )(where, *pieces)


def local(
    queries,
    keys_values,
    prompt_bank,
    prompt_lengths,
    requests,
    w_text,
    q_gain,
    k_gain,
    cq_gain,
    ck_gain,
):
    branch = lax.axis_index("branch")
    z = lax.axis_index("z")
    x = lax.axis_index("x")
    c = lax.axis_index("c")
    where = jnp.stack([branch, z, x, c]).astype(jnp.int32)
    heads, head_dim = q_gain.shape
    slots = heads // (NX * NC)
    scale = math.log2(math.e) / math.sqrt(head_dim)
    tokens = queries.shape[1]
    per_branch, count, width = prompt_bank.shape

    def head_major(values):
        return jnp.transpose(values, (1, 0, 2)).reshape(
            8, slots, values.shape[0], values.shape[2]
        )

    banks = [prompt_bank] + [lax.ppermute(prompt_bank, "branch", ring(4, k)) for k in (1, 2, 3)]
    columns = pick_part(where, requests, banks)

    local_queries = queries[0]
    self_queries = head_major(head_norm(local_queries[..., :head_dim], q_gain).astype(BF16))
    self_queries = self_queries.reshape(8, slots * tokens, 128)
    got = lax.all_to_all(
        jnp.concatenate([self_queries, columns], axis=1), GROUP, 0, 0, tiled=True
    )

    pairs = norm_keys(jnp.transpose(keys_values[0], (1, 0, 2)), k_gain)
    got = after(got, pairs)
    pairs = pairs.reshape(8, slots, keys_values.shape[1], 2 * head_dim)
    pairs = lax.all_to_all(pairs, GROUP, 0, 0, tiled=True)
    gathered = lax.all_gather(got, "z", axis=0)

    part = after(head_major(lax.dynamic_slice_in_dim(w_text, branch * 16, 16, 0)), got)
    moved = [lax.dynamic_index_in_dim(part, z, 0, keepdims=False)]
    for k in range(1, NZ):
        piece = lax.dynamic_index_in_dim(part, (z + k) % NZ, 0, keepdims=False)
        moved.append(lax.ppermute(piece, "z", ring(NZ, k)))
    moved = jnp.stack(moved)
    halves = moved[..., :head_dim], moved[..., head_dim:]
    mine = jnp.where(c == 0, halves[0], halves[1])
    other = lax.ppermute(jnp.where(c == 0, halves[1], halves[0]), "c", ring(NC, 1))
    both = jnp.stack([mine, other])
    next_plane, last_plane = (lax.ppermute(both, "branch", ring(4, k)) for k in (1, -1))
    far_planes = (
        lax.ppermute(next_plane[0], "branch", ring(4, 1)),
        lax.ppermute(last_plane[1], "branch", ring(4, -1)),
    )
    weights = (both, next_plane, *far_planes, last_plane)

    def to_others(pieces):
        return [pieces[0]] + [lax.ppermute(pieces[k], "x", ring(NX, k)) for k in (1, 2, 3)]

    gathered = after(gathered, *weights)
    own = self_part(gathered, pairs, scale)
    total = lax.psum_scatter(own, "z", scatter_dimension=0)

    cross_queries = head_major(head_norm(local_queries[..., head_dim:], cq_gain).astype(BF16))
    cross_queries = lax.all_to_all(after(cross_queries, own), "z", 0, 0, tiled=True)

    parts = to_others(text_part(where, after(gathered, own), weights))
    text = jnp.stack(to_others([text_sum(where, parts, ck_gain)] * NX))
    text = after(text, cross_queries)
    other = lax.ppermute(text, "c", ring(NC, 1))
    cross = cross_part(where, requests, prompt_lengths, cross_queries, text, other, scale)
    cross = [cross[0]] + [lax.ppermute(cross[k], "z", ring(NZ, -k)) for k in range(1, NZ)]
    cross = place_part(where, cross)
    mine = last_part(total)
    mine = lax.all_to_all(mine, GROUP, 0, 0, tiled=True)

    def token_major(values):
        values = values.reshape(heads, tokens, head_dim)
        return jnp.transpose(values, (1, 0, 2)).reshape(1, tokens, heads * head_dim)

    return token_major(mine), cross[None]


def solution(mesh):
    fine = Mesh(mesh.devices.reshape(4, NX, NZ, NC), ("branch", "x", "z", "c"))
    seq = ("x", "z", "c")
    in_specs = (
        P("branch", seq, None, None),
        P("branch", seq, None, None),
        P("branch", seq, None),
        P(),
        P(),
        P(seq, None, None),
        P(),
        P(),
        P(),
        P(),
    )
    out_specs = (P("branch", seq, None), P("branch", seq, None))
    return jax.shard_map(local, mesh=fine, in_specs=in_specs, out_specs=out_specs, check_vma=False)
```

```python
import functools
import math

import jax
import jax.numpy as jnp
from jax import lax
from jax.experimental import pallas as pl
from jax.experimental.pallas import tpu as pltpu
from jax.sharding import Mesh
from jax.sharding import PartitionSpec as P

EPSILON = 1e-06
BF16 = jnp.bfloat16
F32 = jnp.float32
NX, NZ, NC = 4, 8, 2
GROUP = ("x", "c")
SUMS = 16
ROWS = 256
VMEM = 24 << 20
ALL_VMEM = 60 << 20


def head_norm(values, gains):
    values = values.astype(F32)
    return values * lax.rsqrt(jnp.mean(values * values, axis=-1, keepdims=True) + EPSILON) * gains


def ring(size, step):
    return [(i, (i + step) % size) for i in range(size)]


def eye_mask():
    first = lax.broadcasted_iota(jnp.int32, (128, 128), 0)
    return first == lax.broadcasted_iota(jnp.int32, (128, 128), 1)


def self_kernel(q_ref, kv_ref, o_ref, *, rows, keys, scale):
    pairs = kv_ref[...].reshape(1024, 256)
    values = jnp.concatenate([pairs[:, 128:], jnp.ones((1024, 128), BF16)], axis=1)
    queries = q_ref[...].reshape(NZ * ROWS, 128)
    eye = eye_mask()
    for i in range(NZ * ROWS // rows):
        total = None
        for j in range(1024 // keys):
            scores = lax.dot_general(
                queries[i * rows : (i + 1) * rows],
                pairs[j * keys : (j + 1) * keys, :128],
                (((1,), (1,)), ((), ())),
                preferred_element_type=F32,
            )
            powers = jnp.exp2(scores * scale).astype(BF16)
            term = jnp.dot(powers, values[j * keys : (j + 1) * keys], preferred_element_type=F32)
            total = term if total is None else total + term
        for a in range(rows // ROWS):
            piece = total[a * ROWS : (a + 1) * ROWS]
            sums = [
                jnp.sum(jnp.where(eye, piece[b * 128 : (b + 1) * 128, 128:], 0.0), axis=0, keepdims=True)
                for b in range(2)
            ]
            sums = jnp.concatenate(sums + [jnp.zeros((6, 128), F32)], axis=0)
            high = sums.astype(BF16).astype(F32)
            result = jnp.concatenate([high, sums - high, piece[:, :128]], axis=0)
            o_ref[i * rows // ROWS + a, 0] = result.astype(BF16)


def self_part(gathered, pairs, scale):
    slots = pairs.shape[1]
    pairs_count = slots * NZ * ROWS * 1024
    return pl.pallas_call(
        functools.partial(self_kernel, rows=1024, keys=1024, scale=scale),
        grid=(slots,),
        in_specs=[
            pl.BlockSpec((NZ, 8, 32, 128), lambda h: (0, 0, h, 0)),
            pl.BlockSpec((8, 1, 128, 256), lambda h: (0, h, 0, 0)),
        ],
        out_specs=pl.BlockSpec((NZ, 1, SUMS + ROWS, 128), lambda h: (0, h, 0, 0)),
        out_shape=jax.ShapeDtypeStruct((NZ, slots, SUMS + ROWS, 128), BF16),
        compiler_params=pltpu.CompilerParams(vmem_limit_bytes=ALL_VMEM),
        cost_estimate=pl.CostEstimate(
            flops=pairs_count * 128 * 6, bytes_accessed=6 << 20, transcendentals=pairs_count
        ),
        name="self_part",
    )(gathered, pairs)


def last_kernel(total_ref, out_ref):
    eye = eye_mask()
    for h in range(out_ref.shape[1]):
        sums = total_ref[h, :SUMS].astype(F32)
        sums = sums[:8] + sums[8:]
        for b in range(2):
            rows = slice(SUMS + b * 128, SUMS + (b + 1) * 128)
            line = jnp.broadcast_to(sums[b : b + 1], (128, 128))
            column = jnp.sum(jnp.where(eye, line, 0.0), axis=1, keepdims=True)
            value = total_ref[h, rows].astype(F32)
            out_ref[b * 4 : (b + 1) * 4, h] = (value / column).astype(BF16).reshape(4, 32, 128)


def last_part(total):
    slots = total.shape[0]
    return pl.pallas_call(
        last_kernel,
        out_shape=jax.ShapeDtypeStruct((8, slots, 32, 128), BF16),
        compiler_params=pltpu.CompilerParams(vmem_limit_bytes=ALL_VMEM),
        name="last_part",
    )(total)


def norm_kernel(kv_ref, gain_ref, out_ref):
    out_ref[..., :128] = head_norm(kv_ref[..., :128], gain_ref[...]).astype(BF16)
    out_ref[..., 128:] = kv_ref[..., 128:]


def norm_keys(pairs, gains):
    heads, rows, width = pairs.shape
    block = heads // 8
    return pl.pallas_call(
        norm_kernel,
        grid=(8,),
        in_specs=[
            pl.BlockSpec((block, rows, width), lambda g: (g, 0, 0)),
            pl.BlockSpec((block, 1, 128), lambda g: (g, 0, 0)),
        ],
        out_specs=pl.BlockSpec((block, rows, width), lambda g: (g, 0, 0)),
        out_shape=jax.ShapeDtypeStruct(pairs.shape, BF16),
        compiler_params=pltpu.CompilerParams(vmem_limit_bytes=VMEM),
        name="norm_keys",
    )(pairs, gains[:, None, :])


def nothing(*refs):
    del refs


def after(value, *others):
    anywhere = pl.BlockSpec(memory_space=pl.ANY)
    return pl.pallas_call(
        nothing,
        in_specs=[anywhere] * (1 + len(others)),
        out_specs=anywhere,
        out_shape=jax.ShapeDtypeStruct(value.shape, value.dtype),
        input_output_aliases={0: 0},
        name="after",
    )(value, *others)


def pick_kernel(where_ref, requests_ref, b0, b1, b2, b3, out_ref):
    wanted = requests_ref[where_ref[0]]
    per_branch = b0.shape[0]
    plane = lax.rem(where_ref[0] - wanted // per_branch + 4, 4)
    prompt = lax.rem(wanted, per_branch)
    rows = None
    for k, ref in enumerate((b0, b1, b2, b3)):
        for p in range(ref.shape[0]):
            value = ref[p].astype(F32)
            here = jnp.logical_and(plane == k, prompt == p)
            rows = value if rows is None else jnp.where(here, value, rows)
    for x in range(NX):
        blocks = [rows[:, (x * 8 + block) * 128 : (x * 8 + block + 1) * 128] for block in range(8)]
        blocks = jnp.concatenate(blocks, axis=0).astype(BF16)
        for c in range(NC):
            out_ref[x * NC + c] = blocks


def pick_part(where, requests, banks):
    per_branch, count, width = banks[0].shape
    return pl.pallas_call(
        pick_kernel,
        grid_spec=pltpu.PrefetchScalarGridSpec(
            num_scalar_prefetch=2,
            grid=(1,),
            in_specs=[pl.BlockSpec(banks[0].shape, lambda i, w, r: (0, 0, 0))] * 4,
            out_specs=pl.BlockSpec((8, 8 * count, 128), lambda i, w, r: (0, 0, 0)),
        ),
        out_shape=jax.ShapeDtypeStruct((8, 8 * count, 128), BF16),
        compiler_params=pltpu.CompilerParams(vmem_limit_bytes=VMEM),
        name="pick_part",
    )(where, requests, *banks)


def slice_kernel(where_ref, value_ref, *out_refs):
    for k, ref in enumerate(out_refs):
        ref[...] = value_ref[lax.rem(where_ref[1] + k, NZ)]


def slice_part(where, value):
    return pl.pallas_call(
        slice_kernel,
        grid_spec=pltpu.PrefetchScalarGridSpec(
            num_scalar_prefetch=1,
            grid=(1,),
            in_specs=[pl.BlockSpec(value.shape, lambda i, w: (0, 0, 0, 0))],
            out_specs=[pl.BlockSpec(value.shape[1:], lambda i, w: (0, 0, 0))] * NZ,
        ),
        out_shape=[jax.ShapeDtypeStruct(value.shape[1:], BF16)] * NZ,
        compiler_params=pltpu.CompilerParams(vmem_limit_bytes=ALL_VMEM),
        name="slice_part",
    )(where, value)


def text_sum_kernel(where_ref, p0, p1, p2, p3, gain_ref, out_ref):
    total = p0[...].astype(F32)
    for ref in (p1, p2, p3):
        total = total + ref[...].astype(F32)
    keys = head_norm(total, gain_ref[0])
    out_ref[...] = jnp.where(where_ref[3] == 0, keys, total).astype(BF16)


def text_sum(where, parts, gains):
    slots, rows, width = parts[0].shape
    return pl.pallas_call(
        text_sum_kernel,
        grid_spec=pltpu.PrefetchScalarGridSpec(
            num_scalar_prefetch=1,
            grid=(1,),
            in_specs=[pl.BlockSpec((slots, rows, width), lambda i, w: (0, 0, 0))] * 4
            + [pl.BlockSpec((1, slots, 1, width), lambda i, w: (w[1], 0, 0, 0))],
            out_specs=pl.BlockSpec((slots, rows, width), lambda i, w: (0, 0, 0)),
        ),
        out_shape=jax.ShapeDtypeStruct((slots, rows, width), BF16),
        compiler_params=pltpu.CompilerParams(vmem_limit_bytes=VMEM),
        name="text_sum",
    )(where, *parts, gains.reshape(NZ, slots, 1, width))


def text_kernel(where_ref, low_ref, high_ref, w0, w1, w2, w4, w3, o0, o1, o2, o3, held, context, product):
    branch, z, x, c = where_ref[0], where_ref[1], where_ref[2], where_ref[3]
    for k, ref in ((0, w0), (1, w1), (3, w3)):
        held[lax.rem(branch - k + 4, 4)] = ref[...]
    for i, ref in enumerate((w2, w4)):
        held[lax.rem(branch + 2, 4), i] = ref[...]
    for i, ref in enumerate((low_ref, high_ref)):
        rows = ref[...].astype(F32)
        for j in range(4):
            part = rows[:, :, j * 8 : (j + 1) * 8].reshape(512, 128)
            first = (i * 4 + j) * 128
            context[:, first : first + 128] = part.astype(BF16)
    for h in range(held.shape[3]):
        weights = jnp.concatenate(
            [
                held[plane, lax.rem(of_c + c, NC), lax.rem(z - of_z + NZ, NZ), h]
                for of_z in range(NZ)
                for of_c in range(NC)
                for plane in range(4)
            ],
            axis=0,
        )
        result = jnp.dot(context[...], weights, preferred_element_type=F32)
        product[:, h] = result.astype(BF16).reshape(NX, 128, 128)
    for k, ref in enumerate((o0, o1, o2, o3)):
        ref[...] = product[lax.rem(x + k, NX)]


def text_part(where, gathered, weights):
    slots = weights[0].shape[2]
    first = slots
    grid_spec = pltpu.PrefetchScalarGridSpec(
        num_scalar_prefetch=1,
        grid=(1,),
        in_specs=[
            pl.BlockSpec((NZ, 8, 32, 128), lambda i, w: (0, 0, first, 0)),
            pl.BlockSpec((NZ, 8, 32, 128), lambda i, w: (0, 0, first + 1, 0)),
        ]
        + [
            pl.BlockSpec(value.shape, lambda i, w, n=value.ndim: (0,) * n) for value in weights
        ],
        out_specs=[pl.BlockSpec((slots, 128, 128), lambda i, w: (0, 0, 0))] * NX,
        scratch_shapes=[
            pltpu.VMEM((4,) + weights[0].shape, BF16),
            pltpu.VMEM((512, 1024), BF16),
            pltpu.VMEM((NX, slots, 128, 128), BF16),
        ],
    )
    return pl.pallas_call(
        text_kernel,
        grid_spec=grid_spec,
        out_shape=[jax.ShapeDtypeStruct((slots, 128, 128), BF16)] * NX,
        compiler_params=pltpu.CompilerParams(vmem_limit_bytes=ALL_VMEM),
        name="text_part",
    )(where, gathered, gathered, *weights)


def cross_kernel(where_ref, requests_ref, lengths_ref, q_ref, mine_ref, other_ref, o_ref, *, scale):
    entry = lax.broadcasted_iota(jnp.int32, (1, 512), 1)
    of_z = 2 * jnp.bitwise_and(where_ref[2] - (entry >> 7) + NX, NX - 1) + ((entry >> 6) & 1)
    of_x, of_c, of_row = (entry >> 4) & 3, (entry >> 3) & 1, entry & 7
    text_row = ((of_x * NZ + of_z) * NC + of_c) * 8 + of_row
    live = text_row < lengths_ref[requests_ref[where_ref[0]]]
    mine, other = mine_ref[...].reshape(512, 128), other_ref[...].reshape(512, 128)
    first = where_ref[3] == 0
    keys, values = jnp.where(first, mine, other), jnp.where(first, other, mine)
    queries = q_ref[...].reshape(ROWS, 128)
    scores = lax.dot_general(
        queries, keys, (((1,), (1,)), ((), ())), preferred_element_type=F32
    )
    powers = jnp.where(live, jnp.exp2(scores * scale), 0.0)
    weights = powers / jnp.sum(powers, axis=1, keepdims=True)
    result = jnp.dot(weights.astype(BF16), values, preferred_element_type=F32)
    result = result.astype(BF16).reshape(8, 32, 128)
    for of_z in range(NZ):
        o_ref[lax.rem(where_ref[1] - of_z + NZ, NZ), 0] = result[of_z]


def cross_part(where, requests, lengths, queries, mine, other, scale):
    slots = queries.shape[1]
    half = pl.BlockSpec((NX, 1, 128, 128), lambda h, *refs: (0, h, 0, 0))
    grid_spec = pltpu.PrefetchScalarGridSpec(
        num_scalar_prefetch=3,
        grid=(slots,),
        in_specs=[pl.BlockSpec((8, 1, 32, 128), lambda h, *refs: (0, h, 0, 0)), half, half],
        out_specs=pl.BlockSpec((8, 1, 32, 128), lambda h, *refs: (0, h, 0, 0)),
    )
    return pl.pallas_call(
        functools.partial(cross_kernel, scale=scale),
        grid_spec=grid_spec,
        out_shape=jax.ShapeDtypeStruct(queries.shape, BF16),
        compiler_params=pltpu.CompilerParams(vmem_limit_bytes=VMEM),
        name="cross_part",
    )(where, requests, lengths, queries, mine, other)


def place_kernel(where_ref, self_ref, *refs):
    self_out, cross_out = refs[NZ:]
    groups, slots, _, width = self_ref.shape
    for g in range(groups):
        for h in range(slots):
            at = (g * slots + h) * width
            self_out[0, :, at : at + width] = self_ref[g, h]
    for k in range(NZ):
        first = lax.rem(where_ref[1] + k, NZ) * (slots * width)
        for h in range(slots):
            at = pl.multiple_of(first + h * width, 128)
            cross_out[0, :, pl.ds(at, width)] = refs[k][h]


def place_part(where, mine, pieces):
    groups, slots, rows, width = mine.shape
    shape = (1, rows, groups * slots * width)
    return pl.pallas_call(
        place_kernel,
        grid_spec=pltpu.PrefetchScalarGridSpec(
            num_scalar_prefetch=1,
            grid=(1,),
            in_specs=[pl.BlockSpec(mine.shape, lambda i, w: (0, 0, 0, 0))]
            + [pl.BlockSpec((slots, rows, width), lambda i, w: (0, 0, 0))] * NZ,
            out_specs=[pl.BlockSpec(shape, lambda i, w: (0, 0, 0))] * 2,
        ),
        out_shape=[jax.ShapeDtypeStruct(shape, BF16)] * 2,
        compiler_params=pltpu.CompilerParams(vmem_limit_bytes=VMEM),
        name="place_part",
    )(where, mine, *pieces)


def local(
    queries,
    keys_values,
    prompt_bank,
    prompt_lengths,
    requests,
    w_text,
    q_gain,
    k_gain,
    cq_gain,
    ck_gain,
):
    branch = lax.axis_index("branch")
    z = lax.axis_index("z")
    x = lax.axis_index("x")
    c = lax.axis_index("c")
    where = jnp.stack([branch, z, x, c]).astype(jnp.int32)
    heads, head_dim = q_gain.shape
    slots = heads // (NX * NC)
    scale = math.log2(math.e) / math.sqrt(head_dim)
    tokens = queries.shape[1]
    per_branch, count, width = prompt_bank.shape

    def head_major(values):
        return jnp.transpose(values, (1, 0, 2)).reshape(
            8, slots, values.shape[0], values.shape[2]
        )

    banks = [prompt_bank] + [lax.ppermute(prompt_bank, "branch", ring(4, k)) for k in (1, 2, 3)]
    columns = pick_part(where, requests, banks)

    local_queries = queries[0]
    self_queries = head_major(head_norm(local_queries[..., :head_dim], q_gain).astype(BF16))
    self_queries = self_queries.reshape(8, slots * tokens, 128)
    got = lax.all_to_all(
        jnp.concatenate([self_queries, columns], axis=1), GROUP, 0, 0, tiled=True
    )

    pairs = norm_keys(jnp.transpose(keys_values[0], (1, 0, 2)), k_gain)
    got = after(got, pairs)
    pairs = pairs.reshape(8, slots, keys_values.shape[1], 2 * head_dim)
    pairs = lax.all_to_all(pairs, GROUP, 0, 0, tiled=True)
    gathered = lax.all_gather(got, "z", axis=0)

    part = head_major(lax.dynamic_slice_in_dim(w_text, branch * 16, 16, 0))
    moved = slice_part(where, part)
    moved = [moved[0]] + [
        lax.ppermute(after(moved[k], got), "z", ring(NZ, k)) for k in range(1, NZ)
    ]
    moved = jnp.stack(moved)
    halves = moved[..., :head_dim], moved[..., head_dim:]
    mine = jnp.where(c == 0, halves[0], halves[1])
    other = lax.ppermute(jnp.where(c == 0, halves[1], halves[0]), "c", ring(NC, 1))
    both = jnp.stack([mine, other])
    next_plane, last_plane = (lax.ppermute(both, "branch", ring(4, k)) for k in (1, -1))
    far_planes = (
        lax.ppermute(next_plane[0], "branch", ring(4, 1)),
        lax.ppermute(last_plane[1], "branch", ring(4, -1)),
    )
    weights = (both, next_plane, *far_planes, last_plane)

    def to_others(pieces):
        return [pieces[0]] + [lax.ppermute(pieces[k], "x", ring(NX, k)) for k in (1, 2, 3)]

    gathered = after(gathered, *weights)
    own = self_part(gathered, pairs, scale)
    total = lax.psum_scatter(own, "z", scatter_dimension=0)

    cross_queries = head_major(head_norm(local_queries[..., head_dim:], cq_gain).astype(BF16))
    cross_queries = lax.all_to_all(after(cross_queries, own), "z", 0, 0, tiled=True)

    parts = to_others(text_part(where, after(gathered, own), weights))
    text = jnp.stack(to_others([text_sum(where, parts, ck_gain)] * NX))
    text = after(text, cross_queries)
    other = lax.ppermute(text, "c", ring(NC, 1))
    cross = cross_part(where, requests, prompt_lengths, cross_queries, text, other, scale)
    cross = [cross[0]] + [lax.ppermute(cross[k], "z", ring(NZ, -k)) for k in range(1, NZ)]
    mine = last_part(total)
    mine = lax.all_to_all(mine, GROUP, 0, 0, tiled=True)

    return tuple(place_part(where, mine, cross))


def solution(mesh):
    fine = Mesh(mesh.devices.reshape(4, NX, NZ, NC), ("branch", "x", "z", "c"))
    seq = ("x", "z", "c")
    in_specs = (
        P("branch", seq, None, None),
        P("branch", seq, None, None),
        P("branch", seq, None),
        P(),
        P(),
        P(seq, None, None),
        P(),
        P(),
        P(),
        P(),
    )
    out_specs = (P("branch", seq, None), P("branch", seq, None))
    return jax.shard_map(local, mesh=fine, in_specs=in_specs, out_specs=out_specs, check_vma=False)
```

```python
import functools
import math

import jax
import jax.numpy as jnp
from jax import lax
from jax.experimental import pallas as pl
from jax.experimental.pallas import tpu as pltpu
from jax.sharding import Mesh
from jax.sharding import PartitionSpec as P

EPSILON = 1e-06
BF16 = jnp.bfloat16
F32 = jnp.float32
NX, NZ, NC = 4, 8, 2
GROUP = ("x", "c")
SUMS = 16
ROWS = 256
VMEM = 24 << 20
ALL_VMEM = 60 << 20


def head_norm(values, gains):
    values = values.astype(F32)
    return values * lax.rsqrt(jnp.mean(values * values, axis=-1, keepdims=True) + EPSILON) * gains


def ring(size, step):
    return [(i, (i + step) % size) for i in range(size)]


def eye_mask():
    first = lax.broadcasted_iota(jnp.int32, (128, 128), 0)
    return first == lax.broadcasted_iota(jnp.int32, (128, 128), 1)


def self_kernel(q_ref, kv_ref, o_ref, *, rows, keys, scale):
    pairs = kv_ref[...].reshape(1024, 256)
    values = jnp.concatenate([pairs[:, 128:], jnp.ones((1024, 128), BF16)], axis=1)
    queries = q_ref[...].reshape(NZ * ROWS, 128)
    eye = eye_mask()
    for i in range(NZ * ROWS // rows):
        total = None
        for j in range(1024 // keys):
            scores = lax.dot_general(
                queries[i * rows : (i + 1) * rows],
                pairs[j * keys : (j + 1) * keys, :128],
                (((1,), (1,)), ((), ())),
                preferred_element_type=F32,
            )
            powers = jnp.exp2(scores * scale).astype(BF16)
            term = jnp.dot(powers, values[j * keys : (j + 1) * keys], preferred_element_type=F32)
            total = term if total is None else total + term
        for a in range(rows // ROWS):
            piece = total[a * ROWS : (a + 1) * ROWS]
            sums = [
                jnp.sum(jnp.where(eye, piece[b * 128 : (b + 1) * 128, 128:], 0.0), axis=0, keepdims=True)
                for b in range(2)
            ]
            sums = jnp.concatenate(sums + [jnp.zeros((6, 128), F32)], axis=0)
            high = sums.astype(BF16).astype(F32)
            result = jnp.concatenate([high, sums - high, piece[:, :128]], axis=0)
            o_ref[i * rows // ROWS + a, 0] = result.astype(BF16)


def self_part(gathered, pairs, scale):
    slots = pairs.shape[1]
    pairs_count = slots * NZ * ROWS * 1024
    return pl.pallas_call(
        functools.partial(self_kernel, rows=1024, keys=1024, scale=scale),
        grid=(slots,),
        in_specs=[
            pl.BlockSpec((NZ, 8, 32, 128), lambda h: (0, 0, h, 0)),
            pl.BlockSpec((8, 1, 128, 256), lambda h: (0, h, 0, 0)),
        ],
        out_specs=pl.BlockSpec((NZ, 1, SUMS + ROWS, 128), lambda h: (0, h, 0, 0)),
        out_shape=jax.ShapeDtypeStruct((NZ, slots, SUMS + ROWS, 128), BF16),
        compiler_params=pltpu.CompilerParams(vmem_limit_bytes=ALL_VMEM),
        cost_estimate=pl.CostEstimate(
            flops=pairs_count * 128 * 6, bytes_accessed=6 << 20, transcendentals=pairs_count
        ),
        name="self_part",
    )(gathered, pairs)


def last_kernel(total_ref, out_ref):
    eye = eye_mask()
    for h in range(out_ref.shape[1]):
        sums = total_ref[h, :SUMS].astype(F32)
        sums = sums[:8] + sums[8:]
        for b in range(2):
            rows = slice(SUMS + b * 128, SUMS + (b + 1) * 128)
            line = jnp.broadcast_to(sums[b : b + 1], (128, 128))
            column = jnp.sum(jnp.where(eye, line, 0.0), axis=1, keepdims=True)
            value = total_ref[h, rows].astype(F32)
            out_ref[b * 4 : (b + 1) * 4, h] = (value / column).astype(BF16).reshape(4, 32, 128)


def last_part(total):
    slots = total.shape[0]
    return pl.pallas_call(
        last_kernel,
        out_shape=jax.ShapeDtypeStruct((8, slots, 32, 128), BF16),
        compiler_params=pltpu.CompilerParams(vmem_limit_bytes=ALL_VMEM),
        name="last_part",
    )(total)


def norm_kernel(kv_ref, gain_ref, out_ref):
    out_ref[..., :128] = head_norm(kv_ref[..., :128], gain_ref[...]).astype(BF16)
    out_ref[..., 128:] = kv_ref[..., 128:]


def norm_keys(pairs, gains):
    heads, rows, width = pairs.shape
    block = heads // 8
    return pl.pallas_call(
        norm_kernel,
        grid=(8,),
        in_specs=[
            pl.BlockSpec((block, rows, width), lambda g: (g, 0, 0)),
            pl.BlockSpec((block, 1, 128), lambda g: (g, 0, 0)),
        ],
        out_specs=pl.BlockSpec((block, rows, width), lambda g: (g, 0, 0)),
        out_shape=jax.ShapeDtypeStruct(pairs.shape, BF16),
        compiler_params=pltpu.CompilerParams(vmem_limit_bytes=VMEM),
        name="norm_keys",
    )(pairs, gains[:, None, :])


def nothing(*refs):
    del refs


def after(value, *others):
    anywhere = pl.BlockSpec(memory_space=pl.ANY)
    return pl.pallas_call(
        nothing,
        in_specs=[anywhere] * (1 + len(others)),
        out_specs=anywhere,
        out_shape=jax.ShapeDtypeStruct(value.shape, value.dtype),
        input_output_aliases={0: 0},
        name="after",
    )(value, *others)


def choose_kernel(where_ref, requests_ref, bank_ref, *out_refs):
    per_branch = bank_ref.shape[0]
    for k, ref in enumerate(out_refs):
        prompt = lax.rem(requests_ref[lax.rem(where_ref[0] + k, 4)], per_branch)
        rows = bank_ref[0].astype(F32)
        for p in range(1, per_branch):
            rows = jnp.where(prompt == p, bank_ref[p].astype(F32), rows)
        ref[...] = rows.astype(BF16)


def choose_part(where, requests, bank):
    _, count, width = bank.shape
    return pl.pallas_call(
        choose_kernel,
        grid_spec=pltpu.PrefetchScalarGridSpec(
            num_scalar_prefetch=2,
            grid=(1,),
            in_specs=[pl.BlockSpec(bank.shape, lambda i, w, r: (0, 0, 0))],
            out_specs=[pl.BlockSpec((count, width), lambda i, w, r: (0, 0))] * 4,
        ),
        out_shape=[jax.ShapeDtypeStruct((count, width), BF16)] * 4,
        compiler_params=pltpu.CompilerParams(vmem_limit_bytes=VMEM),
        name="choose_part",
    )(where, requests, bank)


def pick_kernel(where_ref, requests_ref, b0, b1, b2, b3, out_ref, *, per_branch):
    wanted = requests_ref[where_ref[0]]
    plane = lax.rem(where_ref[0] - wanted // per_branch + 4, 4)
    rows = b0[...].astype(F32)
    for k, ref in ((1, b1), (2, b2), (3, b3)):
        rows = jnp.where(plane == k, ref[...].astype(F32), rows)
    for x in range(NX):
        blocks = [rows[:, (x * 8 + block) * 128 : (x * 8 + block + 1) * 128] for block in range(8)]
        blocks = jnp.concatenate(blocks, axis=0).astype(BF16)
        for c in range(NC):
            out_ref[x * NC + c] = blocks


def pick_part(where, requests, banks, per_branch):
    count, width = banks[0].shape
    return pl.pallas_call(
        functools.partial(pick_kernel, per_branch=per_branch),
        grid_spec=pltpu.PrefetchScalarGridSpec(
            num_scalar_prefetch=2,
            grid=(1,),
            in_specs=[pl.BlockSpec((count, width), lambda i, w, r: (0, 0))] * 4,
            out_specs=pl.BlockSpec((8, 8 * count, 128), lambda i, w, r: (0, 0, 0)),
        ),
        out_shape=jax.ShapeDtypeStruct((8, 8 * count, 128), BF16),
        compiler_params=pltpu.CompilerParams(vmem_limit_bytes=VMEM),
        name="pick_part",
    )(where, requests, *banks)


def slice_kernel(where_ref, value_ref, *out_refs):
    for k, ref in enumerate(out_refs):
        ref[...] = value_ref[lax.rem(where_ref[1] + k, NZ)]


def slice_part(where, value):
    return pl.pallas_call(
        slice_kernel,
        grid_spec=pltpu.PrefetchScalarGridSpec(
            num_scalar_prefetch=1,
            grid=(1,),
            in_specs=[pl.BlockSpec(value.shape, lambda i, w: (0, 0, 0, 0))],
            out_specs=[pl.BlockSpec(value.shape[1:], lambda i, w: (0, 0, 0))] * NZ,
        ),
        out_shape=[jax.ShapeDtypeStruct(value.shape[1:], BF16)] * NZ,
        compiler_params=pltpu.CompilerParams(vmem_limit_bytes=ALL_VMEM),
        name="slice_part",
    )(where, value)


def text_sum_kernel(where_ref, p0, p1, p2, p3, gain_ref, out_ref):
    total = p0[...].astype(F32)
    for ref in (p1, p2, p3):
        total = total + ref[...].astype(F32)
    keys = head_norm(total, gain_ref[0])
    out_ref[...] = jnp.where(where_ref[3] == 0, keys, total).astype(BF16)


def text_sum(where, parts, gains):
    slots, rows, width = parts[0].shape
    return pl.pallas_call(
        text_sum_kernel,
        grid_spec=pltpu.PrefetchScalarGridSpec(
            num_scalar_prefetch=1,
            grid=(1,),
            in_specs=[pl.BlockSpec((slots, rows, width), lambda i, w: (0, 0, 0))] * 4
            + [pl.BlockSpec((1, slots, 1, width), lambda i, w: (w[1], 0, 0, 0))],
            out_specs=pl.BlockSpec((slots, rows, width), lambda i, w: (0, 0, 0)),
        ),
        out_shape=jax.ShapeDtypeStruct((slots, rows, width), BF16),
        compiler_params=pltpu.CompilerParams(vmem_limit_bytes=VMEM),
        name="text_sum",
    )(where, *parts, gains.reshape(NZ, slots, 1, width))


def text_kernel(where_ref, low_ref, high_ref, w0, w1, w2, w4, w3, o0, o1, o2, o3, held, context, product):
    branch, z, x, c = where_ref[0], where_ref[1], where_ref[2], where_ref[3]
    for k, ref in ((0, w0), (1, w1), (3, w3)):
        held[lax.rem(branch - k + 4, 4)] = ref[...]
    for i, ref in enumerate((w2, w4)):
        held[lax.rem(branch + 2, 4), i] = ref[...]
    for i, ref in enumerate((low_ref, high_ref)):
        rows = ref[...].astype(F32)
        for j in range(4):
            part = rows[:, :, j * 8 : (j + 1) * 8].reshape(512, 128)
            first = (i * 4 + j) * 128
            context[:, first : first + 128] = part.astype(BF16)
    for h in range(held.shape[3]):
        weights = jnp.concatenate(
            [
                held[plane, lax.rem(of_c + c, NC), lax.rem(z - of_z + NZ, NZ), h]
                for of_z in range(NZ)
                for of_c in range(NC)
                for plane in range(4)
            ],
            axis=0,
        )
        result = jnp.dot(context[...], weights, preferred_element_type=F32)
        product[:, h] = result.astype(BF16).reshape(NX, 128, 128)
    for k, ref in enumerate((o0, o1, o2, o3)):
        ref[...] = product[lax.rem(x + k, NX)]


def text_part(where, gathered, weights):
    slots = weights[0].shape[2]
    first = slots
    grid_spec = pltpu.PrefetchScalarGridSpec(
        num_scalar_prefetch=1,
        grid=(1,),
        in_specs=[
            pl.BlockSpec((NZ, 8, 32, 128), lambda i, w: (0, 0, first, 0)),
            pl.BlockSpec((NZ, 8, 32, 128), lambda i, w: (0, 0, first + 1, 0)),
        ]
        + [
            pl.BlockSpec(value.shape, lambda i, w, n=value.ndim: (0,) * n) for value in weights
        ],
        out_specs=[pl.BlockSpec((slots, 128, 128), lambda i, w: (0, 0, 0))] * NX,
        scratch_shapes=[
            pltpu.VMEM((4,) + weights[0].shape, BF16),
            pltpu.VMEM((512, 1024), BF16),
            pltpu.VMEM((NX, slots, 128, 128), BF16),
        ],
    )
    return pl.pallas_call(
        text_kernel,
        grid_spec=grid_spec,
        out_shape=[jax.ShapeDtypeStruct((slots, 128, 128), BF16)] * NX,
        compiler_params=pltpu.CompilerParams(vmem_limit_bytes=ALL_VMEM),
        name="text_part",
    )(where, gathered, gathered, *weights)


def cross_kernel(where_ref, requests_ref, lengths_ref, q_ref, mine_ref, other_ref, o_ref, *, scale):
    entry = lax.broadcasted_iota(jnp.int32, (1, 512), 1)
    of_z = 2 * jnp.bitwise_and(where_ref[2] - (entry >> 7) + NX, NX - 1) + ((entry >> 6) & 1)
    of_x, of_c, of_row = (entry >> 4) & 3, (entry >> 3) & 1, entry & 7
    text_row = ((of_x * NZ + of_z) * NC + of_c) * 8 + of_row
    live = text_row < lengths_ref[requests_ref[where_ref[0]]]
    mine, other = mine_ref[...].reshape(512, 128), other_ref[...].reshape(512, 128)
    first = where_ref[3] == 0
    keys, values = jnp.where(first, mine, other), jnp.where(first, other, mine)
    queries = q_ref[...].reshape(ROWS, 128)
    scores = lax.dot_general(
        queries, keys, (((1,), (1,)), ((), ())), preferred_element_type=F32
    )
    powers = jnp.where(live, jnp.exp2(scores * scale), 0.0)
    weights = powers / jnp.sum(powers, axis=1, keepdims=True)
    result = jnp.dot(weights.astype(BF16), values, preferred_element_type=F32)
    result = result.astype(BF16).reshape(8, 32, 128)
    for of_z in range(NZ):
        o_ref[lax.rem(where_ref[1] - of_z + NZ, NZ), 0] = result[of_z]


def cross_part(where, requests, lengths, queries, mine, other, scale):
    slots = queries.shape[1]
    half = pl.BlockSpec((NX, 1, 128, 128), lambda h, *refs: (0, h, 0, 0))
    grid_spec = pltpu.PrefetchScalarGridSpec(
        num_scalar_prefetch=3,
        grid=(slots,),
        in_specs=[pl.BlockSpec((8, 1, 32, 128), lambda h, *refs: (0, h, 0, 0)), half, half],
        out_specs=pl.BlockSpec((8, 1, 32, 128), lambda h, *refs: (0, h, 0, 0)),
    )
    return pl.pallas_call(
        functools.partial(cross_kernel, scale=scale),
        grid_spec=grid_spec,
        out_shape=jax.ShapeDtypeStruct(queries.shape, BF16),
        compiler_params=pltpu.CompilerParams(vmem_limit_bytes=VMEM),
        name="cross_part",
    )(where, requests, lengths, queries, mine, other)


def queries_kernel(q_ref, self_gain_ref, cross_gain_ref, self_out, cross_out):
    for gain_ref, out_ref, first in ((self_gain_ref, self_out, 0), (cross_gain_ref, cross_out, 128)):
        value = head_norm(q_ref[:, :, first : first + 128], gain_ref[...])
        out_ref[...] = jnp.swapaxes(value, 0, 1).astype(BF16)


def queries_part(queries, self_gain, cross_gain):
    tokens, heads, width = queries.shape
    shape = jax.ShapeDtypeStruct((heads, tokens, width // 2), BF16)
    return pl.pallas_call(
        queries_kernel,
        out_shape=[shape, shape],
        compiler_params=pltpu.CompilerParams(vmem_limit_bytes=ALL_VMEM),
        name="queries_part",
    )(queries, self_gain, cross_gain)


def place_kernel(where_ref, self_ref, *refs):
    self_out, cross_out = refs[NZ:]
    groups, slots, _, width = self_ref.shape
    for g in range(groups):
        for h in range(slots):
            at = (g * slots + h) * width
            self_out[0, :, at : at + width] = self_ref[g, h]
    for k in range(NZ):
        first = lax.rem(where_ref[1] + k, NZ) * (slots * width)
        for h in range(slots):
            at = pl.multiple_of(first + h * width, 128)
            cross_out[0, :, pl.ds(at, width)] = refs[k][h]


def place_part(where, mine, pieces):
    groups, slots, rows, width = mine.shape
    shape = (1, rows, groups * slots * width)
    return pl.pallas_call(
        place_kernel,
        grid_spec=pltpu.PrefetchScalarGridSpec(
            num_scalar_prefetch=1,
            grid=(1,),
            in_specs=[pl.BlockSpec(mine.shape, lambda i, w: (0, 0, 0, 0))]
            + [pl.BlockSpec((slots, rows, width), lambda i, w: (0, 0, 0))] * NZ,
            out_specs=[pl.BlockSpec(shape, lambda i, w: (0, 0, 0))] * 2,
        ),
        out_shape=[jax.ShapeDtypeStruct(shape, BF16)] * 2,
        compiler_params=pltpu.CompilerParams(vmem_limit_bytes=VMEM),
        name="place_part",
    )(where, mine, *pieces)


def local(
    queries,
    keys_values,
    prompt_bank,
    prompt_lengths,
    requests,
    w_text,
    q_gain,
    k_gain,
    cq_gain,
    ck_gain,
):
    branch = lax.axis_index("branch")
    z = lax.axis_index("z")
    x = lax.axis_index("x")
    c = lax.axis_index("c")
    where = jnp.stack([branch, z, x, c]).astype(jnp.int32)
    heads, head_dim = q_gain.shape
    slots = heads // (NX * NC)
    scale = math.log2(math.e) / math.sqrt(head_dim)
    tokens = queries.shape[1]
    per_branch, count, width = prompt_bank.shape

    def head_major(values):
        return jnp.transpose(values, (1, 0, 2)).reshape(
            8, slots, values.shape[0], values.shape[2]
        )

    banks = choose_part(where, requests, prompt_bank)
    banks = [banks[0]] + [lax.ppermute(banks[k], "branch", ring(4, k)) for k in (1, 2, 3)]
    columns = pick_part(where, requests, banks, per_branch)

    local_queries = queries[0]
    self_queries, cross_queries = queries_part(local_queries, q_gain, cq_gain)
    self_queries = self_queries.reshape(8, slots * tokens, 128)
    got = lax.all_to_all(
        jnp.concatenate([self_queries, columns], axis=1), GROUP, 0, 0, tiled=True
    )

    pairs = norm_keys(jnp.transpose(keys_values[0], (1, 0, 2)), k_gain)
    got = after(got, pairs)
    pairs = pairs.reshape(8, slots, keys_values.shape[1], 2 * head_dim)
    pairs = lax.all_to_all(pairs, GROUP, 0, 0, tiled=True)
    gathered = lax.all_gather(got, "z", axis=0)

    part = head_major(lax.dynamic_slice_in_dim(w_text, branch * 16, 16, 0))
    moved = slice_part(where, part)
    moved = [moved[0]] + [
        lax.ppermute(after(moved[k], got), "z", ring(NZ, k)) for k in range(1, NZ)
    ]
    moved = jnp.stack(moved)
    halves = moved[..., :head_dim], moved[..., head_dim:]
    mine = jnp.where(c == 0, halves[0], halves[1])
    other = lax.ppermute(jnp.where(c == 0, halves[1], halves[0]), "c", ring(NC, 1))
    both = jnp.stack([mine, other])
    next_plane, last_plane = (lax.ppermute(both, "branch", ring(4, k)) for k in (1, -1))
    far_planes = (
        lax.ppermute(next_plane[0], "branch", ring(4, 1)),
        lax.ppermute(last_plane[1], "branch", ring(4, -1)),
    )
    weights = (both, next_plane, *far_planes, last_plane)

    def to_others(pieces):
        return [pieces[0]] + [lax.ppermute(pieces[k], "x", ring(NX, k)) for k in (1, 2, 3)]

    gathered = after(gathered, *weights)
    own = self_part(gathered, pairs, scale)
    total = lax.psum_scatter(own, "z", scatter_dimension=0)

    cross_queries = cross_queries.reshape(8, slots, tokens, head_dim)
    cross_queries = lax.all_to_all(after(cross_queries, own), "z", 0, 0, tiled=True)

    parts = to_others(text_part(where, after(gathered, own), weights))
    text = jnp.stack(to_others([text_sum(where, parts, ck_gain)] * NX))
    text = after(text, cross_queries)
    other = lax.ppermute(text, "c", ring(NC, 1))
    cross = cross_part(where, requests, prompt_lengths, cross_queries, text, other, scale)
    cross = [cross[0]] + [lax.ppermute(cross[k], "z", ring(NZ, -k)) for k in range(1, NZ)]
    mine = last_part(total)
    mine = lax.all_to_all(mine, GROUP, 0, 0, tiled=True)

    return tuple(place_part(where, mine, cross))


def solution(mesh):
    fine = Mesh(mesh.devices.reshape(4, NX, NZ, NC), ("branch", "x", "z", "c"))
    seq = ("x", "z", "c")
    in_specs = (
        P("branch", seq, None, None),
        P("branch", seq, None, None),
        P("branch", seq, None),
        P(),
        P(),
        P(seq, None, None),
        P(),
        P(),
        P(),
        P(),
    )
    out_specs = (P("branch", seq, None), P("branch", seq, None))
    return jax.shard_map(local, mesh=fine, in_specs=in_specs, out_specs=out_specs, check_vma=False)
```

```python
import functools
import math

import jax
import jax.numpy as jnp
from jax import lax
from jax.experimental import pallas as pl
from jax.experimental.pallas import tpu as pltpu
from jax.sharding import Mesh
from jax.sharding import PartitionSpec as P

EPSILON = 1e-06
BF16 = jnp.bfloat16
F32 = jnp.float32
NX, NZ, NC = 4, 8, 2
GROUP = ("x", "c")
SUMS = 16
ROWS = 256
VMEM = 24 << 20
ALL_VMEM = 60 << 20


def head_norm(values, gains):
    values = values.astype(F32)
    return values * lax.rsqrt(jnp.mean(values * values, axis=-1, keepdims=True) + EPSILON) * gains


def ring(size, step):
    return [(i, (i + step) % size) for i in range(size)]


def eye_mask():
    first = lax.broadcasted_iota(jnp.int32, (128, 128), 0)
    return first == lax.broadcasted_iota(jnp.int32, (128, 128), 1)


def self_kernel(q_ref, kv_ref, o_ref, *, rows, keys, scale):
    pairs = kv_ref[...].reshape(1024, 256)
    values = jnp.concatenate([pairs[:, 128:], jnp.ones((1024, 128), BF16)], axis=1)
    queries = q_ref[...].reshape(NZ * ROWS, 128)
    eye = eye_mask()
    for i in range(NZ * ROWS // rows):
        total = None
        for j in range(1024 // keys):
            scores = lax.dot_general(
                queries[i * rows : (i + 1) * rows],
                pairs[j * keys : (j + 1) * keys, :128],
                (((1,), (1,)), ((), ())),
                preferred_element_type=F32,
            )
            powers = jnp.exp2(scores * scale).astype(BF16)
            term = jnp.dot(powers, values[j * keys : (j + 1) * keys], preferred_element_type=F32)
            total = term if total is None else total + term
        for a in range(rows // ROWS):
            piece = total[a * ROWS : (a + 1) * ROWS]
            sums = [
                jnp.sum(jnp.where(eye, piece[b * 128 : (b + 1) * 128, 128:], 0.0), axis=0, keepdims=True)
                for b in range(2)
            ]
            sums = jnp.concatenate(sums + [jnp.zeros((6, 128), F32)], axis=0)
            high = sums.astype(BF16).astype(F32)
            result = jnp.concatenate([high, sums - high, piece[:, :128]], axis=0)
            o_ref[i * rows // ROWS + a, 0] = result.astype(BF16)


def self_part(gathered, pairs, scale):
    slots = pairs.shape[1]
    pairs_count = slots * NZ * ROWS * 1024
    return pl.pallas_call(
        functools.partial(self_kernel, rows=1024, keys=1024, scale=scale),
        grid=(slots,),
        in_specs=[
            pl.BlockSpec((NZ, 8, 32, 128), lambda h: (0, 0, h, 0)),
            pl.BlockSpec((8, 1, 128, 256), lambda h: (0, h, 0, 0)),
        ],
        out_specs=pl.BlockSpec((NZ, 1, SUMS + ROWS, 128), lambda h: (0, h, 0, 0)),
        out_shape=jax.ShapeDtypeStruct((NZ, slots, SUMS + ROWS, 128), BF16),
        compiler_params=pltpu.CompilerParams(vmem_limit_bytes=ALL_VMEM),
        cost_estimate=pl.CostEstimate(
            flops=pairs_count * 128 * 6, bytes_accessed=6 << 20, transcendentals=pairs_count
        ),
        name="self_part",
    )(gathered, pairs)


def last_kernel(total_ref, out_ref):
    eye = eye_mask()
    for h in range(out_ref.shape[1]):
        sums = total_ref[h, :SUMS].astype(F32)
        sums = sums[:8] + sums[8:]
        for b in range(2):
            rows = slice(SUMS + b * 128, SUMS + (b + 1) * 128)
            line = jnp.broadcast_to(sums[b : b + 1], (128, 128))
            column = jnp.sum(jnp.where(eye, line, 0.0), axis=1, keepdims=True)
            value = total_ref[h, rows].astype(F32)
            out_ref[b * 4 : (b + 1) * 4, h] = (value / column).astype(BF16).reshape(4, 32, 128)


def last_part(total):
    slots = total.shape[0]
    return pl.pallas_call(
        last_kernel,
        out_shape=jax.ShapeDtypeStruct((8, slots, 32, 128), BF16),
        compiler_params=pltpu.CompilerParams(vmem_limit_bytes=ALL_VMEM),
        name="last_part",
    )(total)


def norm_kernel(kv_ref, gain_ref, out_ref):
    out_ref[..., :128] = head_norm(kv_ref[..., :128], gain_ref[...]).astype(BF16)
    out_ref[..., 128:] = kv_ref[..., 128:]


def norm_keys(pairs, gains):
    heads, rows, width = pairs.shape
    block = heads // 8
    return pl.pallas_call(
        norm_kernel,
        grid=(8,),
        in_specs=[
            pl.BlockSpec((block, rows, width), lambda g: (g, 0, 0)),
            pl.BlockSpec((block, 1, 128), lambda g: (g, 0, 0)),
        ],
        out_specs=pl.BlockSpec((block, rows, width), lambda g: (g, 0, 0)),
        out_shape=jax.ShapeDtypeStruct(pairs.shape, BF16),
        compiler_params=pltpu.CompilerParams(vmem_limit_bytes=VMEM),
        name="norm_keys",
    )(pairs, gains[:, None, :])


def nothing(*refs):
    del refs


def after(value, *others):
    anywhere = pl.BlockSpec(memory_space=pl.ANY)
    return pl.pallas_call(
        nothing,
        in_specs=[anywhere] * (1 + len(others)),
        out_specs=anywhere,
        out_shape=jax.ShapeDtypeStruct(value.shape, value.dtype),
        input_output_aliases={0: 0},
        name="after",
    )(value, *others)


def pick_kernel(where_ref, requests_ref, b0, b1, b2, b3, out_ref):
    wanted = requests_ref[where_ref[0]]
    per_branch = b0.shape[0]
    plane = lax.rem(where_ref[0] - wanted // per_branch + 4, 4)
    prompt = lax.rem(wanted, per_branch)
    rows = None
    for k, ref in enumerate((b0, b1, b2, b3)):
        for p in range(ref.shape[0]):
            value = ref[p].astype(F32)
            here = jnp.logical_and(plane == k, prompt == p)
            rows = value if rows is None else jnp.where(here, value, rows)
    for x in range(NX):
        blocks = [rows[:, (x * 8 + block) * 128 : (x * 8 + block + 1) * 128] for block in range(8)]
        blocks = jnp.concatenate(blocks, axis=0).astype(BF16)
        for c in range(NC):
            out_ref[x * NC + c] = blocks


def pick_part(where, requests, banks):
    per_branch, count, width = banks[0].shape
    return pl.pallas_call(
        pick_kernel,
        grid_spec=pltpu.PrefetchScalarGridSpec(
            num_scalar_prefetch=2,
            grid=(1,),
            in_specs=[pl.BlockSpec(banks[0].shape, lambda i, w, r: (0, 0, 0))] * 4,
            out_specs=pl.BlockSpec((8, 8 * count, 128), lambda i, w, r: (0, 0, 0)),
        ),
        out_shape=jax.ShapeDtypeStruct((8, 8 * count, 128), BF16),
        compiler_params=pltpu.CompilerParams(vmem_limit_bytes=VMEM),
        name="pick_part",
    )(where, requests, *banks)


def slice_kernel(where_ref, value_ref, *out_refs):
    for k, ref in enumerate(out_refs):
        ref[...] = value_ref[lax.rem(where_ref[1] + k, NZ)]


def slice_part(where, value):
    return pl.pallas_call(
        slice_kernel,
        grid_spec=pltpu.PrefetchScalarGridSpec(
            num_scalar_prefetch=1,
            grid=(1,),
            in_specs=[pl.BlockSpec(value.shape, lambda i, w: (0, 0, 0, 0))],
            out_specs=[pl.BlockSpec(value.shape[1:], lambda i, w: (0, 0, 0))] * NZ,
        ),
        out_shape=[jax.ShapeDtypeStruct(value.shape[1:], BF16)] * NZ,
        compiler_params=pltpu.CompilerParams(vmem_limit_bytes=ALL_VMEM),
        name="slice_part",
    )(where, value)


def text_sum_kernel(where_ref, p0, p1, p2, p3, gain_ref, out_ref):
    total = p0[...].astype(F32)
    for ref in (p1, p2, p3):
        total = total + ref[...].astype(F32)
    keys = head_norm(total, gain_ref[0])
    out_ref[...] = jnp.where(where_ref[3] == 0, keys, total).astype(BF16)


def text_sum(where, parts, gains):
    slots, rows, width = parts[0].shape
    return pl.pallas_call(
        text_sum_kernel,
        grid_spec=pltpu.PrefetchScalarGridSpec(
            num_scalar_prefetch=1,
            grid=(1,),
            in_specs=[pl.BlockSpec((slots, rows, width), lambda i, w: (0, 0, 0))] * 4
            + [pl.BlockSpec((1, slots, 1, width), lambda i, w: (w[1], 0, 0, 0))],
            out_specs=pl.BlockSpec((slots, rows, width), lambda i, w: (0, 0, 0)),
        ),
        out_shape=jax.ShapeDtypeStruct((slots, rows, width), BF16),
        compiler_params=pltpu.CompilerParams(vmem_limit_bytes=ALL_VMEM),
        name="text_sum",
    )(where, *parts, gains.reshape(NZ, slots, 1, width))


def text_kernel(where_ref, low_ref, high_ref, w0, w1, w2, w4, w3, o0, o1, o2, o3, held, context, product):
    branch, z, x, c = where_ref[0], where_ref[1], where_ref[2], where_ref[3]
    for k, ref in ((0, w0), (1, w1), (3, w3)):
        held[lax.rem(branch - k + 4, 4)] = ref[...]
    for i, ref in enumerate((w2, w4)):
        held[lax.rem(branch + 2, 4), i] = ref[...]
    for i, ref in enumerate((low_ref, high_ref)):
        rows = ref[...].astype(F32)
        for j in range(4):
            part = rows[:, :, j * 8 : (j + 1) * 8].reshape(512, 128)
            first = (i * 4 + j) * 128
            context[:, first : first + 128] = part.astype(BF16)
    for h in range(held.shape[3]):
        weights = jnp.concatenate(
            [
                held[plane, lax.rem(of_c + c, NC), lax.rem(z - of_z + NZ, NZ), h]
                for of_z in range(NZ)
                for of_c in range(NC)
                for plane in range(4)
            ],
            axis=0,
        )
        result = jnp.dot(context[...], weights, preferred_element_type=F32)
        product[:, h] = result.astype(BF16).reshape(NX, 128, 128)
    for k, ref in enumerate((o0, o1, o2, o3)):
        ref[...] = product[lax.rem(x + k, NX)]


def text_part(where, gathered, weights):
    slots = weights[0].shape[2]
    first = slots
    grid_spec = pltpu.PrefetchScalarGridSpec(
        num_scalar_prefetch=1,
        grid=(1,),
        in_specs=[
            pl.BlockSpec((NZ, 8, 32, 128), lambda i, w: (0, 0, first, 0)),
            pl.BlockSpec((NZ, 8, 32, 128), lambda i, w: (0, 0, first + 1, 0)),
        ]
        + [
            pl.BlockSpec(value.shape, lambda i, w, n=value.ndim: (0,) * n) for value in weights
        ],
        out_specs=[pl.BlockSpec((slots, 128, 128), lambda i, w: (0, 0, 0))] * NX,
        scratch_shapes=[
            pltpu.VMEM((4,) + weights[0].shape, BF16),
            pltpu.VMEM((512, 1024), BF16),
            pltpu.VMEM((NX, slots, 128, 128), BF16),
        ],
    )
    return pl.pallas_call(
        text_kernel,
        grid_spec=grid_spec,
        out_shape=[jax.ShapeDtypeStruct((slots, 128, 128), BF16)] * NX,
        compiler_params=pltpu.CompilerParams(vmem_limit_bytes=ALL_VMEM),
        name="text_part",
    )(where, gathered, gathered, *weights)


def cross_kernel(where_ref, requests_ref, lengths_ref, q_ref, mine_ref, other_ref, o_ref, *, scale):
    entry = lax.broadcasted_iota(jnp.int32, (1, 512), 1)
    of_z = 2 * jnp.bitwise_and(where_ref[2] - (entry >> 7) + NX, NX - 1) + ((entry >> 6) & 1)
    of_x, of_c, of_row = (entry >> 4) & 3, (entry >> 3) & 1, entry & 7
    text_row = ((of_x * NZ + of_z) * NC + of_c) * 8 + of_row
    live = text_row < lengths_ref[requests_ref[where_ref[0]]]
    mine, other = mine_ref[...].reshape(512, 128), other_ref[...].reshape(512, 128)
    first = where_ref[3] == 0
    keys, values = jnp.where(first, mine, other), jnp.where(first, other, mine)
    queries = q_ref[...].reshape(ROWS, 128)
    scores = lax.dot_general(
        queries, keys, (((1,), (1,)), ((), ())), preferred_element_type=F32
    )
    powers = jnp.where(live, jnp.exp2(scores * scale), 0.0)
    weights = powers / jnp.sum(powers, axis=1, keepdims=True)
    result = jnp.dot(weights.astype(BF16), values, preferred_element_type=F32)
    result = result.astype(BF16).reshape(8, 32, 128)
    for of_z in range(NZ):
        o_ref[lax.rem(where_ref[1] - of_z + NZ, NZ), 0] = result[of_z]


def cross_part(where, requests, lengths, queries, mine, other, scale):
    slots = queries.shape[1]
    half = pl.BlockSpec((NX, 1, 128, 128), lambda h, *refs: (0, h, 0, 0))
    grid_spec = pltpu.PrefetchScalarGridSpec(
        num_scalar_prefetch=3,
        grid=(slots,),
        in_specs=[pl.BlockSpec((8, 1, 32, 128), lambda h, *refs: (0, h, 0, 0)), half, half],
        out_specs=pl.BlockSpec((8, 1, 32, 128), lambda h, *refs: (0, h, 0, 0)),
    )
    return pl.pallas_call(
        functools.partial(cross_kernel, scale=scale),
        grid_spec=grid_spec,
        out_shape=jax.ShapeDtypeStruct(queries.shape, BF16),
        compiler_params=pltpu.CompilerParams(vmem_limit_bytes=ALL_VMEM),
        name="cross_part",
    )(where, requests, lengths, queries, mine, other)


def place_kernel(where_ref, self_ref, *refs):
    self_out, cross_out = refs[NZ:]
    groups, slots, _, width = self_ref.shape
    for g in range(groups):
        for h in range(slots):
            at = (g * slots + h) * width
            self_out[0, :, at : at + width] = self_ref[g, h]
    for k in range(NZ):
        first = lax.rem(where_ref[1] + k, NZ) * (slots * width)
        for h in range(slots):
            at = pl.multiple_of(first + h * width, 128)
            cross_out[0, :, pl.ds(at, width)] = refs[k][h]


def place_part(where, mine, pieces):
    groups, slots, rows, width = mine.shape
    shape = (1, rows, groups * slots * width)
    return pl.pallas_call(
        place_kernel,
        grid_spec=pltpu.PrefetchScalarGridSpec(
            num_scalar_prefetch=1,
            grid=(1,),
            in_specs=[pl.BlockSpec(mine.shape, lambda i, w: (0, 0, 0, 0))]
            + [pl.BlockSpec((slots, rows, width), lambda i, w: (0, 0, 0))] * NZ,
            out_specs=[pl.BlockSpec(shape, lambda i, w: (0, 0, 0))] * 2,
        ),
        out_shape=[jax.ShapeDtypeStruct(shape, BF16)] * 2,
        compiler_params=pltpu.CompilerParams(vmem_limit_bytes=VMEM),
        name="place_part",
    )(where, mine, *pieces)


def local(
    queries,
    keys_values,
    prompt_bank,
    prompt_lengths,
    requests,
    w_text,
    q_gain,
    k_gain,
    cq_gain,
    ck_gain,
):
    branch = lax.axis_index("branch")
    z = lax.axis_index("z")
    x = lax.axis_index("x")
    c = lax.axis_index("c")
    where = jnp.stack([branch, z, x, c]).astype(jnp.int32)
    heads, head_dim = q_gain.shape
    slots = heads // (NX * NC)
    scale = math.log2(math.e) / math.sqrt(head_dim)
    tokens = queries.shape[1]
    per_branch, count, width = prompt_bank.shape

    def head_major(values):
        return jnp.transpose(values, (1, 0, 2)).reshape(
            8, slots, values.shape[0], values.shape[2]
        )

    banks = [prompt_bank] + [lax.ppermute(prompt_bank, "branch", ring(4, k)) for k in (1, 2, 3)]
    columns = pick_part(where, requests, banks)

    local_queries = queries[0]
    self_queries = head_major(head_norm(local_queries[..., :head_dim], q_gain).astype(BF16))
    self_queries = self_queries.reshape(8, slots * tokens, 128)
    got = lax.all_to_all(
        jnp.concatenate([self_queries, columns], axis=1), GROUP, 0, 0, tiled=True
    )

    pairs = norm_keys(jnp.transpose(keys_values[0], (1, 0, 2)), k_gain)
    got = after(got, pairs)
    pairs = pairs.reshape(8, slots, keys_values.shape[1], 2 * head_dim)
    pairs = lax.all_to_all(pairs, GROUP, 0, 0, tiled=True)
    gathered = lax.all_gather(got, "z", axis=0)

    part = head_major(lax.dynamic_slice_in_dim(w_text, branch * 16, 16, 0))
    moved = slice_part(where, part)
    moved = [moved[0]] + [
        lax.ppermute(after(moved[k], got), "z", ring(NZ, k)) for k in range(1, NZ)
    ]
    moved = jnp.stack(moved)
    halves = moved[..., :head_dim], moved[..., head_dim:]
    mine = jnp.where(c == 0, halves[0], halves[1])
    other = lax.ppermute(jnp.where(c == 0, halves[1], halves[0]), "c", ring(NC, 1))
    both = jnp.stack([mine, other])
    next_plane, last_plane = (lax.ppermute(both, "branch", ring(4, k)) for k in (1, -1))
    far_planes = (
        lax.ppermute(next_plane[0], "branch", ring(4, 1)),
        lax.ppermute(last_plane[1], "branch", ring(4, -1)),
    )
    weights = (both, next_plane, *far_planes, last_plane)

    def to_others(pieces):
        return [pieces[0]] + [lax.ppermute(pieces[k], "x", ring(NX, k)) for k in (1, 2, 3)]

    gathered = after(gathered, *weights)
    own = self_part(gathered, pairs, scale)
    total = lax.psum_scatter(own, "z", scatter_dimension=0)

    cross_queries = head_major(head_norm(local_queries[..., head_dim:], cq_gain).astype(BF16))
    cross_queries = lax.all_to_all(after(cross_queries, own), "z", 0, 0, tiled=True)

    parts = to_others(text_part(where, after(gathered, own), weights))
    text = jnp.stack(to_others([text_sum(where, parts, ck_gain)] * NX))
    text = after(text, cross_queries)
    other = lax.ppermute(text, "c", ring(NC, 1))
    cross = cross_part(where, requests, prompt_lengths, cross_queries, text, other, scale)
    cross = [cross[0]] + [lax.ppermute(cross[k], "z", ring(NZ, -k)) for k in range(1, NZ)]
    mine = last_part(total)
    mine = lax.all_to_all(mine, GROUP, 0, 0, tiled=True)

    return tuple(place_part(where, mine, cross))


def solution(mesh):
    fine = Mesh(mesh.devices.reshape(4, NX, NZ, NC), ("branch", "x", "z", "c"))
    seq = ("x", "z", "c")
    in_specs = (
        P("branch", seq, None, None),
        P("branch", seq, None, None),
        P("branch", seq, None),
        P(),
        P(),
        P(seq, None, None),
        P(),
        P(),
        P(),
        P(),
    )
    out_specs = (P("branch", seq, None), P("branch", seq, None))
    return jax.shard_map(local, mesh=fine, in_specs=in_specs, out_specs=out_specs, check_vma=False)
```
